32 devices in a mesh: fsdp: 8 (over z, y), tp: 4 (over x, core).
Axes of the slice: x: 2, y: 2, z: 4, core: 2. Of those that a mesh axis runs over, the one named last changes fastest.
Arguments:
- tokens: bfloat16 [8192, 2048], P(('fsdp', 'tp')), may hold values from -6 to 6
- out_grad: bfloat16 [8192, 2048], P(('fsdp', 'tp')), may hold values from -6 to 6
- lengths: int32 [8], P('fsdp'), may hold values from 256 to 1024, as said below
- w_query: float32 [2048, 2048], P('fsdp', 'tp'), may hold values from -0.125 to 0.125
- w_key: float32 [2048, 1024], P('fsdp', 'tp'), may hold values from -0.125 to 0.125
- w_value: float32 [2048, 1024], P('fsdp', 'tp'), may hold values from -0.125 to 0.125
- w_out: float32 [2048, 2048], P('fsdp', 'tp'), may hold values from -3 to 3
- w_gate: float32 [2048, 8192], P('fsdp', 'tp'), may hold values from -0.125 to 0.125
- w_up: float32 [2048, 8192], P('fsdp', 'tp'), may hold values from -0.125 to 0.125
- w_down: float32 [2048, 8192], P('fsdp', 'tp'), may hold values from -0.0625 to 0.0625
- norm_attn: float32 [2048], replicated, may hold values from 0.5 to 1.5
- norm_mlp: float32 [2048], replicated, may hold values from 0.5 to 1.5
- moment_query: float32 [2048, 2048], P('fsdp', 'tp'), may hold values from -7.6293945e-05 to 7.6293945e-05
- moment_key: float32 [2048, 1024], P('fsdp', 'tp'), may hold values from -7.6293945e-05 to 7.6293945e-05
- moment_value: float32 [2048, 1024], P('fsdp', 'tp'), may hold values from -7.6293945e-05 to 7.6293945e-05
- moment_out: float32 [2048, 2048], P('fsdp', 'tp'), may hold values from -1.5258789e-05 to 1.5258789e-05
- moment_gate: float32 [2048, 8192], P('fsdp', 'tp'), may hold values from -7.6293945e-05 to 7.6293945e-05
- moment_up: float32 [2048, 8192], P('fsdp', 'tp'), may hold values from -7.6293945e-05 to 7.6293945e-05
- moment_down: float32 [2048, 8192], P('fsdp', 'tp'), may hold values from -7.6293945e-05 to 7.6293945e-05
- moment_norm_attn: float32 [2048], replicated, may hold values from -7.6293945e-05 to 7.6293945e-05
- moment_norm_mlp: float32 [2048], replicated, may hold values from -7.6293945e-05 to 7.6293945e-05
- square_query: float32 [2048, 2048], P('fsdp', 'tp'), may hold values from 1.5893538e-10 to 1.5893538e-09
- square_key: float32 [2048, 1024], P('fsdp', 'tp'), may hold values from 1.5893538e-10 to 1.5893538e-09
- square_value: float32 [2048, 1024], P('fsdp', 'tp'), may hold values from 1.5893538e-10 to 1.5893538e-09
- square_out: float32 [2048, 2048], P('fsdp', 'tp'), may hold values from 4.768061e-12 to 4.7680613e-11
- square_gate: float32 [2048, 8192], P('fsdp', 'tp'), may hold values from 1.5893538e-10 to 1.5893538e-09
- square_up: float32 [2048, 8192], P('fsdp', 'tp'), may hold values from 1.5893538e-10 to 1.5893538e-09
- square_down: float32 [2048, 8192], P('fsdp', 'tp'), may hold values from 1.5893538e-10 to 1.5893538e-09
- square_norm_attn: float32 [2048], replicated, may hold values from 1.5893538e-10 to 1.5893538e-09
- square_norm_mlp: float32 [2048], replicated, may hold values from 1.5893538e-10 to 1.5893538e-09
Outputs:
- block_out: bfloat16 [8192, 2048], P(('fsdp', 'tp'))
- input_grad: float32 [8192, 2048], P(('fsdp', 'tp'))
- grad_query: float32 [2048, 2048], P('fsdp', 'tp')
- grad_key: float32 [2048, 1024], P('fsdp', 'tp')
- grad_value: float32 [2048, 1024], P('fsdp', 'tp')
- grad_out_proj: float32 [2048, 2048], P('fsdp', 'tp')
- grad_gate: float32 [2048, 8192], P('fsdp', 'tp')
- grad_up: float32 [2048, 8192], P('fsdp', 'tp')
- grad_down: float32 [2048, 8192], P('fsdp', 'tp')
- grad_norm_attn: float32 [2048], replicated
- grad_norm_mlp: float32 [2048], replicated
- new_moment_query: float32 [2048, 2048], P('fsdp', 'tp')
- new_moment_key: float32 [2048, 1024], P('fsdp', 'tp')
- new_moment_value: float32 [2048, 1024], P('fsdp', 'tp')
- new_moment_out: float32 [2048, 2048], P('fsdp', 'tp')
- new_moment_gate: float32 [2048, 8192], P('fsdp', 'tp')
- new_moment_up: float32 [2048, 8192], P('fsdp', 'tp')
- new_moment_down: float32 [2048, 8192], P('fsdp', 'tp')
- new_moment_norm_attn: float32 [2048], replicated
- new_moment_norm_mlp: float32 [2048], replicated
- new_square_query: float32 [2048, 2048], P('fsdp', 'tp')
- new_square_key: float32 [2048, 1024], P('fsdp', 'tp')
- new_square_value: float32 [2048, 1024], P('fsdp', 'tp')
- new_square_out: float32 [2048, 2048], P('fsdp', 'tp')
- new_square_gate: float32 [2048, 8192], P('fsdp', 'tp')
- new_square_up: float32 [2048, 8192], P('fsdp', 'tp')
- new_square_down: float32 [2048, 8192], P('fsdp', 'tp')
- new_square_norm_attn: float32 [2048], replicated
- new_square_norm_mlp: float32 [2048], replicated
- update_query: float32 [2048, 2048], P('fsdp', 'tp')
- update_key: float32 [2048, 1024], P('fsdp', 'tp')
- update_value: float32 [2048, 1024], P('fsdp', 'tp')
- update_out: float32 [2048, 2048], P('fsdp', 'tp')
- update_gate: float32 [2048, 8192], P('fsdp', 'tp')
- update_up: float32 [2048, 8192], P('fsdp', 'tp')
- update_down: float32 [2048, 8192], P('fsdp', 'tp')
- update_norm_attn: float32 [2048], replicated
- update_norm_mlp: float32 [2048], replicated
- clip_norm: float32 [], replicated
The draws below stay inside these ranges and needn't reach their ends.
Inputs may be any that keep to these rules, and one draw needn't show every extreme that they name: `lengths`: some slot holds a sequence of 1024 tokens and some slot one of a quarter of 1024.
All inputs are finite; a program needn't handle non-finite values.
Results may differ from the reference program's by a relative error of at most 0.02.
The reference program's roundings to bfloat16 on the way count: a program that leaves them out, or rounds other values in their place, can miss the bound.
Values may be sent and summed in bfloat16 or wider, within the bound.
No kernel may reach another device: no remote copies, remote signals or barrier semaphores. Data moves between devices by JAX's collectives and lax.ppermute only.
A program may use at most 168 MiB of HBM per device.

```python
import math
import jax
import jax.numpy as jnp
from jax import lax

D = 2048
HQ = 8
HK = 4
HD = 256
FF = 8192
SLOT = 1024
STEP = 10
SLOTS = 8
TOKENS = 8192
PARAMS = 62918656


def draw_lengths(key, part):
    first_key, second_key, third_key = jax.random.split(key, 3)
    drawn = jax.random.randint(first_key, (SLOTS,), SLOT // 4, SLOT + 1)
    longest = jax.random.randint(second_key, (), 0, SLOTS)
    shortest = (longest + 1 + jax.random.randint(third_key, (), 0, SLOTS - 1)) % SLOTS
    places = jnp.arange(SLOTS)
    drawn = jnp.where(places == longest, SLOT, drawn)
    return jnp.where(places == shortest, SLOT // 4, drawn).astype(jnp.int32)


def steps_of(rng, extent, cuts, least, top_value):
    level = 1.0
    for position, shards_of in cuts:
        steps = jax.random.uniform(jax.random.fold_in(jax.random.fold_in(rng, 6), position), (shards_of,), jnp.float32, least / len(cuts), top_value / len(cuts))
        level = level * jnp.repeat(jnp.exp(steps), extent[position] // shards_of).reshape((-1,) + (1,) * (len(extent) - 1 - position))
    return level


def noise(rng, extent, scale, limit, cuts=(), held_as=jnp.bfloat16):
    array = jax.random.normal(rng, extent, jnp.float32) * scale
    if len(cuts) > 0:
        array = steps_of(rng, extent, cuts, -0.22, 0.18) * array
    return jnp.clip(array, min=-limit, max=limit).astype(held_as)


def setup_inputs(seed: int = 0) -> dict:
    arg_keys = jax.random.split(jax.random.key(seed), 31)
    return {
        "tokens": noise(arg_keys[0], (TOKENS, D), 1.0, 6.0, ((0, 32),)),
        "out_grad": noise(arg_keys[1], (TOKENS, D), 1.0, 6.0, ((0, 32),)),
        "lengths": draw_lengths(jax.random.fold_in(arg_keys[30], 71), 0),
        "w_query": noise(arg_keys[3], (D, HQ * HD), D ** -0.5, 0.125, ((0, 8), (1, 4)), jnp.float32),
        "w_key": noise(arg_keys[4], (D, HK * HD), D ** -0.5, 0.125, ((0, 8), (1, 4)), jnp.float32),
        "w_value": noise(arg_keys[5], (D, HK * HD), D ** -0.5, 0.125, ((0, 8), (1, 4)), jnp.float32),
        "w_out": noise(arg_keys[6], (D, HQ * HD), (max(1, HQ * HD * 2 // SLOT)) ** -0.5, 3.0, ((0, 8), (1, 4)), jnp.float32),
        "w_gate": noise(arg_keys[7], (D, FF), D ** -0.5, 0.125, ((0, 8), (1, 4)), jnp.float32),
        "w_up": noise(arg_keys[8], (D, FF), D ** -0.5, 0.125, ((0, 8), (1, 4)), jnp.float32),
        "w_down": noise(arg_keys[9], (D, FF), FF ** -0.5, 0.0625, ((0, 8), (1, 4)), jnp.float32),
        "norm_attn": jnp.clip(1.0 + 0.1 * jax.random.normal(arg_keys[10], (D,), jnp.float32), 0.5, 1.5),
        "norm_mlp": jnp.clip(1.0 + 0.1 * jax.random.normal(arg_keys[11], (D,), jnp.float32), 0.5, 1.5),
        "moment_query": noise(arg_keys[12], (D, HQ * HD), (0.1 / PARAMS ** 0.5), 7.62939453125e-05, ((0, 8), (1, 4)), jnp.float32),
        "moment_key": noise(arg_keys[13], (D, HK * HD), (0.1 / PARAMS ** 0.5), 7.62939453125e-05, ((0, 8), (1, 4)), jnp.float32),
        "moment_value": noise(arg_keys[14], (D, HK * HD), (0.1 / PARAMS ** 0.5), 7.62939453125e-05, ((0, 8), (1, 4)), jnp.float32),
        "moment_out": noise(arg_keys[15], (D, HQ * HD), (0.02 / PARAMS ** 0.5), 1.52587890625e-05, ((0, 8), (1, 4)), jnp.float32),
        "moment_gate": noise(arg_keys[16], (D, FF), (0.1 / PARAMS ** 0.5), 7.62939453125e-05, ((0, 8), (1, 4)), jnp.float32),
        "moment_up": noise(arg_keys[17], (D, FF), (0.1 / PARAMS ** 0.5), 7.62939453125e-05, ((0, 8), (1, 4)), jnp.float32),
        "moment_down": noise(arg_keys[18], (D, FF), (0.1 / PARAMS ** 0.5), 7.62939453125e-05, ((0, 8), (1, 4)), jnp.float32),
        "moment_norm_attn": noise(arg_keys[19], (D,), (0.1 / PARAMS ** 0.5), 7.62939453125e-05, (), jnp.float32),
        "moment_norm_mlp": noise(arg_keys[20], (D,), (0.1 / PARAMS ** 0.5), 7.62939453125e-05, (), jnp.float32),
        "square_query": jnp.clip(jnp.exp(math.log(1.5893537597122531e-09) - 2.3025851 * jax.random.uniform(arg_keys[21], (D, HQ * HD), jnp.float32) ** steps_of(arg_keys[21], (D, HQ * HD), ((0, 8), (1, 4)), -0.2, 0.2)), 1.5893537874678287e-10, 1.5893537597122531e-09),
        "square_key": jnp.clip(jnp.exp(math.log(1.5893537597122531e-09) - 2.3025851 * jax.random.uniform(arg_keys[22], (D, HK * HD), jnp.float32) ** steps_of(arg_keys[22], (D, HK * HD), ((0, 8), (1, 4)), -0.2, 0.2)), 1.5893537874678287e-10, 1.5893537597122531e-09),
        "square_value": jnp.clip(jnp.exp(math.log(1.5893537597122531e-09) - 2.3025851 * jax.random.uniform(arg_keys[23], (D, HK * HD), jnp.float32) ** steps_of(arg_keys[23], (D, HK * HD), ((0, 8), (1, 4)), -0.2, 0.2)), 1.5893537874678287e-10, 1.5893537597122531e-09),
        "square_out": jnp.clip(jnp.exp(math.log(4.768061293014547e-11) - 2.3025852 * jax.random.uniform(arg_keys[24], (D, HQ * HD), jnp.float32) ** steps_of(arg_keys[24], (D, HQ * HD), ((0, 8), (1, 4)), -0.2, 0.2)), 4.768060946069852e-12, 4.768061293014547e-11),
        "square_gate": jnp.clip(jnp.exp(math.log(1.5893537597122531e-09) - 2.3025851 * jax.random.uniform(arg_keys[25], (D, FF), jnp.float32) ** steps_of(arg_keys[25], (D, FF), ((0, 8), (1, 4)), -0.2, 0.2)), 1.5893537874678287e-10, 1.5893537597122531e-09),
        "square_up": jnp.clip(jnp.exp(math.log(1.5893537597122531e-09) - 2.3025851 * jax.random.uniform(arg_keys[26], (D, FF), jnp.float32) ** steps_of(arg_keys[26], (D, FF), ((0, 8), (1, 4)), -0.2, 0.2)), 1.5893537874678287e-10, 1.5893537597122531e-09),
        "square_down": jnp.clip(jnp.exp(math.log(1.5893537597122531e-09) - 2.3025851 * jax.random.uniform(arg_keys[27], (D, FF), jnp.float32) ** steps_of(arg_keys[27], (D, FF), ((0, 8), (1, 4)), -0.2, 0.2)), 1.5893537874678287e-10, 1.5893537597122531e-09),
        "square_norm_attn": jnp.clip(jnp.exp(jax.random.uniform(arg_keys[28], (D,), jnp.float32, math.log(1.5893537874678287e-10), math.log(1.5893537597122531e-09))), 1.5893537874678287e-10, 1.5893537597122531e-09),
        "square_norm_mlp": jnp.clip(jnp.exp(jax.random.uniform(arg_keys[29], (D,), jnp.float32, math.log(1.5893537874678287e-10), math.log(1.5893537597122531e-09))), 1.5893537874678287e-10, 1.5893537597122531e-09),
    }


EPS_NORM = 1e-05
THETA = 1000042.0
LEARN_RATE = 0.02
BETA_ONE = 0.9
BETA_TWO = 0.95
ADAM_EPS = 1e-08
WEIGHT_DECAY = 0.1
MAX_NORM = 1.0
MASKED = -1000000000.0

@jax.custom_vjp
def low(v):
    return lax.optimization_barrier(v.astype(jnp.bfloat16)).astype(jnp.float32)

@jax.custom_vjp
def low_back(v):
    return v

def low_keep(v):
    return (low(v), None)

def low_pass(kept, grad):
    return (grad,)

def back_keep(v):
    return (v, None)

def back_low(kept, grad):
    return (low(grad),)
low.defvjp(low_keep, low_pass)
low_back.defvjp(back_keep, back_low)

def matmul(left, right):
    return jnp.dot(left, right, precision=lax.Precision.HIGHEST, preferred_element_type=jnp.float32)

def matmul_t(left, right):
    return lax.dot_general(left, right, (((1,), (1,)), ((), ())), precision=lax.Precision.HIGHEST, preferred_element_type=jnp.float32)

def rms_scale(values, norm_gain):
    return values * lax.rsqrt(lax.optimization_barrier(jnp.mean(values * values, axis=-1, keepdims=True)) + EPS_NORM) * norm_gain

def rotary_tables(count, head_dim):
    positions = jnp.arange(count).astype(jnp.float32)
    inverse = THETA ** (-2.0 * jnp.arange(head_dim // 2).astype(jnp.float32) / head_dim)
    angles = positions[:, None] * inverse[None, :]
    return (jnp.cos(angles)[:, None, :], jnp.sin(angles)[:, None, :])

def rotary(values, cosine_table, sine_table):
    half_width = values.shape[-1] // 2
    first_half = values[..., :half_width]
    second_half = values[..., half_width:]
    return jnp.concatenate([first_half * cosine_table - second_half * sine_table, second_half * cosine_table + first_half * sine_table], axis=-1)

def slot_forward(resid_in, length, weights, norm_attn, norm_mlp, cosine_table, sine_table):
    w_query, w_key, w_value, w_out, w_gate, w_up, w_down = weights
    positions = jnp.arange(SLOT)
    normed_attn = low(rms_scale(resid_in, norm_attn))
    query_lin = low_back(matmul(normed_attn, w_query)).reshape(SLOT, HQ, HD)
    key_lin = low_back(matmul(normed_attn, w_key)).reshape(SLOT, HK, HD)
    value_low = low(low_back(matmul(normed_attn, w_value))).reshape(SLOT, HK, HD)
    query_rot = low(rotary(query_lin, cosine_table, sine_table)).reshape(SLOT, HK, HQ // HK, HD)
    key_rot = low(rotary(key_lin, cosine_table, sine_table))
    raw_scores = low_back(jnp.einsum('qkgd,skd->kgqs', query_rot, key_rot, precision=lax.Precision.HIGHEST, preferred_element_type=jnp.float32))
    allowed = (positions[None, :] <= positions[:, None]) & (positions[None, :] < length)
    scores = jnp.where(allowed, raw_scores * HD ** (-0.5), MASKED)
    row_peak = lax.optimization_barrier(jnp.max(scores, axis=-1, keepdims=True))
    exponent = jnp.exp(scores - row_peak)
    attn_probs = low(exponent / lax.optimization_barrier(jnp.sum(exponent, axis=-1, keepdims=True)))
    attended = jnp.einsum('kgqs,skd->qkgd', attn_probs, value_low, precision=lax.Precision.HIGHEST, preferred_element_type=jnp.float32)
    attn_low = low(low_back(attended.reshape(SLOT, HQ * HD)))
    middle = resid_in + low_back(matmul_t(attn_low, w_out))
    normed_mlp = low(rms_scale(middle, norm_mlp))
    gate_lin = low_back(matmul(normed_mlp, w_gate))
    up_lin = low_back(matmul(normed_mlp, w_up))
    hidden = low(gate_lin * jax.nn.sigmoid(gate_lin) * up_lin)
    return middle + low_back(matmul_t(hidden, w_down))

def adam_step(master, gradient, moment, square, factor):
    clipped = gradient * factor
    new_moment = BETA_ONE * moment + (1.0 - BETA_ONE) * clipped
    new_square = BETA_TWO * square + (1.0 - BETA_TWO) * clipped * clipped
    moment_hat = new_moment / (1.0 - BETA_ONE ** STEP)
    square_hat = new_square / (1.0 - BETA_TWO ** STEP)
    update = -LEARN_RATE * (moment_hat / (jnp.sqrt(square_hat) + ADAM_EPS) + WEIGHT_DECAY * master)
    return (new_moment, new_square, update)

def reference(tokens, out_grad, lengths, w_query, w_key, w_value, w_out, w_gate, w_up, w_down, norm_attn, norm_mlp, moment_query, moment_key, moment_value, moment_out, moment_gate, moment_up, moment_down, moment_norm_attn, moment_norm_mlp, square_query, square_key, square_value, square_out, square_gate, square_up, square_down, square_norm_attn, square_norm_mlp):
    masters = (w_query, w_key, w_value, w_out, w_gate, w_up, w_down)
    cosine_table, sine_table = rotary_tables(SLOT, HD)

    def forward(resid_all, master_list, gain_attn, gain_mlp):
        weights = tuple((low(master) for master in master_list))

        def one_slot(scan_carry, slot_item):
            resid_slot, length = slot_item
            out_slot = jax.checkpoint(slot_forward)(resid_slot, length, weights, gain_attn, gain_mlp, cosine_table, sine_table)
            return (scan_carry, out_slot)
        _, slot_outs = lax.scan(one_slot, jnp.zeros((), jnp.float32), (resid_all.reshape(SLOTS, SLOT, D), lengths))
        return slot_outs.reshape(TOKENS, D)
    block_f32, pullback = jax.vjp(forward, tokens.astype(jnp.float32), masters, norm_attn, norm_mlp)
    row_valid = (jnp.arange(SLOT)[None, :] < lengths[:, None]).reshape(TOKENS).astype(jnp.float32)
    cotangent = out_grad.astype(jnp.float32) * row_valid[:, None]
    input_grad, master_grads, grad_norm_attn, grad_norm_mlp = pullback(cotangent)
    every_grad = tuple(master_grads) + (grad_norm_attn, grad_norm_mlp)
    square_total = jnp.zeros((), jnp.float32)
    for gradient in every_grad:
        square_total = square_total + jnp.sum(gradient * gradient)
    clip_norm = jnp.sqrt(square_total)
    factor = jnp.minimum(1.0, MAX_NORM / (clip_norm + 1e-06))
    params = masters + (norm_attn, norm_mlp)
    moments = (moment_query, moment_key, moment_value, moment_out, moment_gate, moment_up, moment_down, moment_norm_attn, moment_norm_mlp)
    squares = (square_query, square_key, square_value, square_out, square_gate, square_up, square_down, square_norm_attn, square_norm_mlp)
    results = [adam_step(params[number], every_grad[number], moments[number], squares[number], factor) for number in range(9)]
    return (block_f32.astype(jnp.bfloat16), input_grad, every_grad[0], every_grad[1], every_grad[2], every_grad[3], every_grad[4], every_grad[5], every_grad[6], every_grad[7], every_grad[8], results[0][0], results[1][0], results[2][0], results[3][0], results[4][0], results[5][0], results[6][0], results[7][0], results[8][0], results[0][1], results[1][1], results[2][1], results[3][1], results[4][1], results[5][1], results[6][1], results[7][1], results[8][1], results[0][2], results[1][2], results[2][2], results[3][2], results[4][2], results[5][2], results[6][2], results[7][2], results[8][2], clip_norm)
```

```python
import jax
import jax.numpy as jnp
from jax import lax
from jax.sharding import PartitionSpec as P

HD = 256
STEP = 10


EPS_NORM = 1e-05
THETA = 1000042.0
LEARN_RATE = 0.02
BETA_ONE = 0.9
BETA_TWO = 0.95
ADAM_EPS = 1e-08
WEIGHT_DECAY = 0.1
MAX_NORM = 1.0
MASKED = -1000000000.0


def rms_scale(values, norm_gain):
    return (
        values * lax.rsqrt(jnp.mean(values * values, axis=-1, keepdims=True) + EPS_NORM) * norm_gain
    )


def norm_back(values, norm_gain, incoming):
    row_scale = lax.rsqrt(jnp.mean(values * values, axis=-1, keepdims=True) + EPS_NORM)
    weighted = incoming * norm_gain
    grad_values = row_scale * weighted - values * row_scale**3 * jnp.mean(
        weighted * values, axis=-1, keepdims=True
    )
    return (grad_values, jnp.sum(incoming * values * row_scale, axis=0))


def rotary_tables(count, head_dim):
    positions = jnp.arange(count).astype(jnp.float32)
    inverse = THETA ** (-2.0 * jnp.arange(head_dim // 2).astype(jnp.float32) / head_dim)
    angles = positions[:, None] * inverse[None, :]
    return (jnp.cos(angles)[:, None, :], jnp.sin(angles)[:, None, :])


def rotary(values, cosine_table, sine_table):
    half_width = values.shape[-1] // 2
    first_half = values[..., :half_width]
    second_half = values[..., half_width:]
    return jnp.concatenate(
        [
            first_half * cosine_table - second_half * sine_table,
            second_half * cosine_table + first_half * sine_table,
        ],
        axis=-1,
    )


def dot_rows(left, right):
    return lax.dot_general(
        left, right, (((0,), (0,)), ((), ())), preferred_element_type=jnp.float32
    )


def dot_last(left, right):
    return lax.dot_general(
        left, right, (((1,), (1,)), ((), ())), preferred_element_type=jnp.float32
    )


def block_mask(first_row, block_rows, slot_rows, length):
    query_pos = first_row + jnp.arange(block_rows)
    key_pos = jnp.arange(slot_rows)
    return (key_pos[None, :] <= query_pos[:, None]) & (key_pos[None, :] < length)


def attend(query_rot, key_rot, value_bf, length, block_rows, heads_kv):
    slot_rows = query_rot.shape[0]
    head_dim = query_rot.shape[-1]
    group_size = query_rot.shape[1] // heads_kv
    score_scale = head_dim ** (-0.5)

    def one_block(block_index):
        first_row = block_index * block_rows
        query_blk = lax.dynamic_slice_in_dim(query_rot, first_row, block_rows, 0).reshape(
            block_rows, heads_kv, group_size, head_dim
        )
        raw_scores = jnp.einsum(
            "qkgd,skd->kgqs", query_blk, key_rot, preferred_element_type=jnp.float32
        )
        allowed = block_mask(first_row, block_rows, slot_rows, length)
        scores = jnp.where(allowed, raw_scores * score_scale, MASKED)
        row_peak = jnp.max(scores, axis=-1, keepdims=True)
        exponent = jnp.exp(scores - row_peak)
        row_total = jnp.sum(exponent, axis=-1, keepdims=True)
        attn_probs = (exponent / row_total).astype(jnp.bfloat16)
        attended = jnp.einsum(
            "kgqs,skd->qkgd", attn_probs, value_bf, preferred_element_type=jnp.float32
        )
        return (
            attended.reshape(block_rows, heads_kv * group_size * head_dim),
            (row_peak + jnp.log(row_total))[..., 0],
        )

    attended, log_sums = lax.map(one_block, jnp.arange(slot_rows // block_rows))
    return (attended.reshape(slot_rows, -1), log_sums)


def attend_back(
    query_rot, key_rot, value_bf, attended_grad, log_sums, length, block_rows, heads_kv
):
    slot_rows = query_rot.shape[0]
    head_dim = query_rot.shape[-1]
    group_size = query_rot.shape[1] // heads_kv
    score_scale = head_dim ** (-0.5)

    def one_block(carried, block_index):
        key_grad, value_grad = carried
        first_row = block_index * block_rows
        query_blk = lax.dynamic_slice_in_dim(query_rot, first_row, block_rows, 0).reshape(
            block_rows, heads_kv, group_size, head_dim
        )
        grad_blk = lax.dynamic_slice_in_dim(attended_grad, first_row, block_rows, 0).reshape(
            block_rows, heads_kv, group_size, head_dim
        )
        raw_scores = jnp.einsum(
            "qkgd,skd->kgqs", query_blk, key_rot, preferred_element_type=jnp.float32
        )
        allowed = block_mask(first_row, block_rows, slot_rows, length)
        scores = jnp.where(allowed, raw_scores * score_scale, MASKED)
        attn_probs = jnp.exp(scores - log_sums[block_index][..., None])
        prob_grad = jnp.einsum(
            "qkgd,skd->kgqs", grad_blk, value_bf, preferred_element_type=jnp.float32
        )
        row_delta = jnp.sum(attn_probs * prob_grad, axis=-1, keepdims=True)
        score_grad = (attn_probs * (prob_grad - row_delta) * score_scale).astype(jnp.bfloat16)
        query_grad = jnp.einsum(
            "kgqs,skd->qkgd", score_grad, key_rot, preferred_element_type=jnp.float32
        )
        key_grad = key_grad + jnp.einsum(
            "kgqs,qkgd->skd", score_grad, query_blk, preferred_element_type=jnp.float32
        )
        value_grad = value_grad + jnp.einsum(
            "kgqs,qkgd->skd",
            attn_probs.astype(jnp.bfloat16),
            grad_blk,
            preferred_element_type=jnp.float32,
        )
        return (
            (key_grad, value_grad),
            query_grad.reshape(block_rows, heads_kv * group_size, head_dim),
        )

    zero_grads = jnp.zeros(key_rot.shape, jnp.float32)
    (key_grad, value_grad), query_grad = lax.scan(
        one_block, (zero_grads, zero_grads), jnp.arange(slot_rows // block_rows)
    )
    return (query_grad.reshape(slot_rows, heads_kv * group_size, head_dim), key_grad, value_grad)


def adam_step(master, gradient, moment, square, factor):
    clipped = gradient * factor
    new_moment = BETA_ONE * moment + (1.0 - BETA_ONE) * clipped
    new_square = BETA_TWO * square + (1.0 - BETA_TWO) * clipped * clipped
    moment_hat = new_moment / (1.0 - BETA_ONE**STEP)
    square_hat = new_square / (1.0 - BETA_TWO**STEP)
    update = -LEARN_RATE * (moment_hat / (jnp.sqrt(square_hat) + ADAM_EPS) + WEIGHT_DECAY * master)
    return (new_moment, new_square, update)


AXES = ("fsdp", "tp")
PAIR = 2


def swap(value, fsdp_mask, tp_mask, odd_masks=None):
    fsdp_ways, tp_ways = lax.axis_size("fsdp"), lax.axis_size("tp")
    pairs = []
    for row in range(fsdp_ways):
        for col in range(tp_ways):
            masks = (fsdp_mask, tp_mask)
            if odd_masks is not None and col & 1:
                masks = odd_masks
            pairs.append((row * tp_ways + col, (row ^ masks[0]) * tp_ways + (col ^ masks[1])))
    return lax.ppermute(value, AXES, pairs)


def bits_below(ways):
    return [1 << power for power in reversed(range(ways.bit_length() - 1))]


def gather_chunks(first, bits):
    chunks = dict(first)
    for bit in bits:
        arrived = {mask ^ bit: swap(chunk, bit, 0) for mask, chunk in chunks.items()}
        chunks.update(arrived)
    return chunks


def assemble(chunks):
    me = lax.axis_index("fsdp")
    rows, cols = chunks[0].shape
    whole = jnp.zeros((rows * len(chunks), cols), chunks[0].dtype)
    for mask, chunk in chunks.items():
        whole = lax.dynamic_update_slice_in_dim(whole, chunk, (me ^ mask) * rows, 0)
    return whole


def scatter_chunks(whole, bits, rows):
    me = lax.axis_index("fsdp")
    ways = whole.shape[0] // rows
    parts = {
        mask: lax.dynamic_slice_in_dim(whole, (me ^ mask) * rows, rows, 0) for mask in range(ways)
    }
    for bit in bits:
        kept = {}
        for mask, part in parts.items():
            if not mask & bit:
                got = swap(parts[mask ^ bit].astype(jnp.bfloat16), bit, 0)
                kept[mask] = part.astype(jnp.float32) + got.astype(jnp.float32)
        parts = kept
    return parts


def gather_slot(block):
    other = swap(block, 0, 2)
    near = swap(block, 0, 1)
    far = swap(other, 0, 1)
    me = lax.axis_index("tp")
    rows = block.shape[0]
    whole = jnp.zeros((rows * 4, block.shape[1]), block.dtype)
    for mask, chunk in ((0, block), (2, other), (1, near), (3, far)):
        whole = lax.dynamic_update_slice_in_dim(whole, chunk, (me ^ mask) * rows, 0)
    return whole


def scatter_slot(whole):
    me = lax.axis_index("tp")
    rows = whole.shape[0] // 4
    parts = [lax.dynamic_slice_in_dim(whole, (me ^ mask) * rows, rows, 0) for mask in range(4)]
    far = parts[2] + swap(parts[3].astype(jnp.bfloat16), 0, 1).astype(jnp.float32)
    own = parts[0] + swap(parts[1].astype(jnp.bfloat16), 0, 1).astype(jnp.float32)
    return own + swap(far.astype(jnp.bfloat16), 0, 2).astype(jnp.float32)


def swap_one(value):
    return swap(value, 0, 2, (PAIR, 0))


def swap_two(value):
    return swap(value, PAIR, 0, (0, 2))


def gather_group(block):
    first = swap_one(block)
    second = swap_two(block)
    both = swap_two(first)
    mine = [block, first, second, both]
    return jnp.concatenate(mine + [swap(each, 0, 1) for each in mine], axis=0)


def scatter_group(whole):
    rows = whole.shape[0] // 8
    parts = [whole[rows * number : rows * (number + 1)] for number in range(8)]
    sums = [
        parts[number].astype(jnp.float32)
        + swap(parts[number + 4].astype(jnp.bfloat16), 0, 1).astype(jnp.float32)
        for number in (3, 2, 1, 0)
    ][::-1]
    first = sums[1] + swap_two(sums[3].astype(jnp.bfloat16)).astype(jnp.float32)
    own = sums[0] + swap_two(sums[2].astype(jnp.bfloat16)).astype(jnp.float32)
    return own + swap_one(first.astype(jnp.bfloat16)).astype(jnp.float32)


def sum_everywhere(value):
    for bit in bits_below(lax.axis_size("tp"))[::-1]:
        value = value + swap(value, 0, bit)
    for bit in bits_below(lax.axis_size("fsdp")):
        value = value + swap(value, bit, 0)
    return value


def half_columns(value, which):
    width = value.shape[1] // 2
    return lax.dynamic_slice_in_dim(value, which * width, width, 1)


def on_device(
    tokens,
    out_grad,
    lengths,
    w_query,
    w_key,
    w_value,
    w_out,
    w_gate,
    w_up,
    w_down,
    norm_attn,
    norm_mlp,
    moment_query,
    moment_key,
    moment_value,
    moment_out,
    moment_gate,
    moment_up,
    moment_down,
    moment_norm_attn,
    moment_norm_mlp,
    square_query,
    square_key,
    square_value,
    square_out,
    square_gate,
    square_up,
    square_down,
    square_norm_attn,
    square_norm_mlp,
):
    rows_dev = tokens.shape[0]
    tp_ways = lax.axis_size("tp")
    fsdp_ways = lax.axis_size("fsdp")
    all_bits = bits_below(fsdp_ways)
    far_bits = [bit for bit in all_bits if bit != PAIR]
    pair_side = (lax.axis_index("fsdp") // PAIR) % 2
    slot_rows = rows_dev * tp_ways
    block_rows = min(512, slot_rows)
    heads_kv = w_key.shape[1] // HD
    weight_rows = w_query.shape[0]
    length = lengths[0]
    row_pos = lax.axis_index("tp") * rows_dev + jnp.arange(rows_dev)
    row_valid = (row_pos < length).astype(jnp.float32)
    cosine_table, sine_table = rotary_tables(slot_rows, HD)
    resid_in = tokens.astype(jnp.float32)
    normed_attn = rms_scale(resid_in, norm_attn).astype(jnp.bfloat16)
    low_qkv = jnp.concatenate([w_query, w_key, w_value], axis=1).astype(jnp.bfloat16)
    low_out = w_out.astype(jnp.bfloat16)
    full_qkv = assemble(gather_chunks({0: low_qkv}, all_bits))
    attn_input = gather_slot(normed_attn)
    full_out = assemble(gather_chunks({0: low_out}, all_bits))

    def gather_wide(weight):
        kept = half_columns(weight, pair_side).astype(jnp.bfloat16)
        sent = half_columns(weight, 1 - pair_side).astype(jnp.bfloat16)
        return assemble(gather_chunks({0: kept, PAIR: swap(sent, PAIR, 0)}, far_bits))

    def scatter_wide(gradient):
        parts = scatter_chunks(gradient, far_bits[::-1], weight_rows)
        got = swap(parts[PAIR].astype(jnp.bfloat16), PAIR, 0).astype(jnp.float32)
        return jnp.where(
            pair_side == 0,
            jnp.concatenate([parts[0], got], axis=1),
            jnp.concatenate([got, parts[0]], axis=1),
        )

    full_gate = gather_wide(w_gate)
    full_up = gather_wide(w_up)
    full_down = gather_wide(w_down)
    cotangent = out_grad.astype(jnp.float32) * row_valid[:, None]
    mlp_grad_in = gather_group(cotangent.astype(jnp.bfloat16))

    width_query, width_key = w_query.shape[1], w_key.shape[1]
    qkv_lin = jnp.dot(attn_input, full_qkv, preferred_element_type=jnp.float32)
    query_lin = qkv_lin[:, :width_query].reshape(slot_rows, -1, HD)
    key_lin = qkv_lin[:, width_query : width_query + width_key].reshape(slot_rows, heads_kv, HD)
    value_bf = (
        qkv_lin[:, width_query + width_key :].astype(jnp.bfloat16).reshape(slot_rows, heads_kv, HD)
    )
    query_rot = rotary(query_lin, cosine_table, sine_table).astype(jnp.bfloat16)
    key_rot = rotary(key_lin, cosine_table, sine_table).astype(jnp.bfloat16)
    attended, log_sums = attend(query_rot, key_rot, value_bf, length, block_rows, heads_kv)
    attn_bf = attended.astype(jnp.bfloat16)
    middle = resid_in + scatter_slot(dot_last(attn_bf, full_out))
    normed_mlp = rms_scale(middle, norm_mlp).astype(jnp.bfloat16)
    mlp_input = gather_group(normed_mlp)
    gate_lin = jnp.dot(mlp_input, full_gate, preferred_element_type=jnp.float32)
    up_lin = jnp.dot(mlp_input, full_up, preferred_element_type=jnp.float32)
    gate_sig = jax.nn.sigmoid(gate_lin)
    hidden_bf = (gate_lin * gate_sig * up_lin).astype(jnp.bfloat16)
    grad_down = dot_rows(mlp_grad_in, hidden_bf)
    shard_down = scatter_wide(grad_down.astype(jnp.bfloat16))
    hidden_grad = jnp.dot(mlp_grad_in, full_down, preferred_element_type=jnp.float32)
    gate_grad = (hidden_grad * up_lin * gate_sig * (1.0 + gate_lin * (1.0 - gate_sig))).astype(
        jnp.bfloat16
    )
    up_grad = (hidden_grad * gate_lin * gate_sig).astype(jnp.bfloat16)
    normed_mlp_grad = scatter_group(dot_last(gate_grad, full_gate) + dot_last(up_grad, full_up))
    shard_gate = scatter_wide(dot_rows(mlp_input, gate_grad).astype(jnp.bfloat16))
    shard_up = scatter_wide(dot_rows(mlp_input, up_grad).astype(jnp.bfloat16))
    middle_back, gain_mlp_part = norm_back(middle, norm_mlp, normed_mlp_grad)
    middle_grad = cotangent + middle_back
    attn_grad_in = gather_slot(middle_grad.astype(jnp.bfloat16))
    attended_grad = jnp.dot(attn_grad_in, full_out, preferred_element_type=jnp.float32).astype(
        jnp.bfloat16
    )
    query_grad_rot, key_grad_rot, value_grad = attend_back(
        query_rot, key_rot, value_bf, attended_grad, log_sums, length, block_rows, heads_kv
    )
    query_grad = rotary(query_grad_rot, cosine_table, -sine_table).reshape(slot_rows, -1)
    key_grad = rotary(key_grad_rot, cosine_table, -sine_table).reshape(slot_rows, -1)
    qkv_grad = jnp.concatenate(
        [query_grad, key_grad, value_grad.reshape(slot_rows, -1)], axis=1
    ).astype(jnp.bfloat16)
    shard_qkv = scatter_chunks(dot_rows(attn_input, qkv_grad), all_bits[::-1], weight_rows)[0]
    shard_out = scatter_chunks(dot_rows(attn_grad_in, attn_bf), all_bits[::-1], weight_rows)[0]
    normed_attn_grad = scatter_slot(dot_last(qkv_grad, full_qkv))
    input_back, gain_attn_part = norm_back(resid_in, norm_attn, normed_attn_grad)
    input_grad = middle_grad + input_back
    block_out = (middle + scatter_group(dot_last(hidden_bf, full_down))).astype(jnp.bfloat16)
    shard_grads = (
        shard_qkv[:, :width_query],
        shard_qkv[:, width_query : width_query + width_key],
        shard_qkv[:, width_query + width_key :],
        shard_out,
        shard_gate,
        shard_up,
        shard_down,
    )
    square_part = jnp.zeros((), jnp.float32)
    for shard_grad in shard_grads:
        square_part = square_part + jnp.sum(shard_grad * shard_grad)
    summed = sum_everywhere(
        jnp.concatenate([gain_attn_part, gain_mlp_part, jnp.broadcast_to(square_part, (128,))])
    )
    gain_attn_grad = summed[: norm_attn.shape[0]]
    gain_mlp_grad = summed[norm_attn.shape[0] : -128]
    square_total = summed[-1]
    clip_norm = jnp.sqrt(
        square_total
        + jnp.sum(gain_attn_grad * gain_attn_grad)
        + jnp.sum(gain_mlp_grad * gain_mlp_grad)
    )
    factor = jnp.minimum(1.0, MAX_NORM / (clip_norm + 1e-06))
    every_grad = tuple(shard_grads) + (gain_attn_grad, gain_mlp_grad)
    params = (w_query, w_key, w_value, w_out, w_gate, w_up, w_down, norm_attn, norm_mlp)
    moments = (
        moment_query,
        moment_key,
        moment_value,
        moment_out,
        moment_gate,
        moment_up,
        moment_down,
        moment_norm_attn,
        moment_norm_mlp,
    )
    squares = (
        square_query,
        square_key,
        square_value,
        square_out,
        square_gate,
        square_up,
        square_down,
        square_norm_attn,
        square_norm_mlp,
    )
    results = [
        adam_step(params[number], every_grad[number], moments[number], squares[number], factor)
        for number in range(9)
    ]
    return (
        block_out,
        input_grad,
        every_grad[0],
        every_grad[1],
        every_grad[2],
        every_grad[3],
        every_grad[4],
        every_grad[5],
        every_grad[6],
        every_grad[7],
        every_grad[8],
        results[0][0],
        results[1][0],
        results[2][0],
        results[3][0],
        results[4][0],
        results[5][0],
        results[6][0],
        results[7][0],
        results[8][0],
        results[0][1],
        results[1][1],
        results[2][1],
        results[3][1],
        results[4][1],
        results[5][1],
        results[6][1],
        results[7][1],
        results[8][1],
        results[0][2],
        results[1][2],
        results[2][2],
        results[3][2],
        results[4][2],
        results[5][2],
        results[6][2],
        results[7][2],
        results[8][2],
        clip_norm,
    )


def solution(mesh):
    return jax.shard_map(
        on_device,
        mesh=mesh,
        in_specs=(
            P(("fsdp", "tp"), None),
            P(("fsdp", "tp"), None),
            P("fsdp"),
            P("fsdp", "tp"),
            P("fsdp", "tp"),
            P("fsdp", "tp"),
            P("fsdp", "tp"),
            P("fsdp", "tp"),
            P("fsdp", "tp"),
            P("fsdp", "tp"),
            P(),
            P(),
            P("fsdp", "tp"),
            P("fsdp", "tp"),
            P("fsdp", "tp"),
            P("fsdp", "tp"),
            P("fsdp", "tp"),
            P("fsdp", "tp"),
            P("fsdp", "tp"),
            P(),
            P(),
            P("fsdp", "tp"),
            P("fsdp", "tp"),
            P("fsdp", "tp"),
            P("fsdp", "tp"),
            P("fsdp", "tp"),
            P("fsdp", "tp"),
            P("fsdp", "tp"),
            P(),
            P(),
        ),
        out_specs=(
            P(("fsdp", "tp"), None),
            P(("fsdp", "tp"), None),
            P("fsdp", "tp"),
            P("fsdp", "tp"),
            P("fsdp", "tp"),
            P("fsdp", "tp"),
            P("fsdp", "tp"),
            P("fsdp", "tp"),
            P("fsdp", "tp"),
            P(),
            P(),
            P("fsdp", "tp"),
            P("fsdp", "tp"),
            P("fsdp", "tp"),
            P("fsdp", "tp"),
            P("fsdp", "tp"),
            P("fsdp", "tp"),
            P("fsdp", "tp"),
            P(),
            P(),
            P("fsdp", "tp"),
            P("fsdp", "tp"),
            P("fsdp", "tp"),
            P("fsdp", "tp"),
            P("fsdp", "tp"),
            P("fsdp", "tp"),
            P("fsdp", "tp"),
            P(),
            P(),
            P("fsdp", "tp"),
            P("fsdp", "tp"),
            P("fsdp", "tp"),
            P("fsdp", "tp"),
            P("fsdp", "tp"),
            P("fsdp", "tp"),
            P("fsdp", "tp"),
            P(),
            P(),
            P(),
        ),
        check_vma=False,
    )
```

```python
import functools

import jax
import jax.numpy as jnp
from jax import lax
from jax.experimental import pallas as pl
from jax.experimental.pallas import tpu as pltpu
from jax.sharding import PartitionSpec as P

HD = 256
STEP = 10


EPS_NORM = 1e-05
THETA = 1000042.0
LEARN_RATE = 0.02
BETA_ONE = 0.9
BETA_TWO = 0.95
ADAM_EPS = 1e-08
WEIGHT_DECAY = 0.1
MAX_NORM = 1.0
MASKED = -1000000000.0


def rotary_tables(count, head_dim):
    positions = jnp.arange(count).astype(jnp.float32)
    inverse = THETA ** (-2.0 * jnp.arange(head_dim // 2).astype(jnp.float32) / head_dim)
    angles = positions[:, None] * inverse[None, :]
    return (jnp.cos(angles), jnp.sin(angles))


def dot_rows(left, right):
    return lax.dot_general(
        left, right, (((0,), (0,)), ((), ())), preferred_element_type=jnp.float32
    )


def dot_last(left, right):
    return lax.dot_general(
        left, right, (((1,), (1,)), ((), ())), preferred_element_type=jnp.float32
    )


def adam_step(master, gradient, moment, square, factor):
    clipped = gradient * factor
    new_moment = BETA_ONE * moment + (1.0 - BETA_ONE) * clipped
    new_square = BETA_TWO * square + (1.0 - BETA_TWO) * clipped * clipped
    moment_hat = new_moment / (1.0 - BETA_ONE**STEP)
    square_hat = new_square / (1.0 - BETA_TWO**STEP)
    update = -LEARN_RATE * (moment_hat / (jnp.sqrt(square_hat) + ADAM_EPS) + WEIGHT_DECAY * master)
    return (new_moment, new_square, update)


F32, BF16 = jnp.float32, jnp.bfloat16
TILE = 256
VMEM_BYTES = 48 * 1024 * 1024
SMALL_COST = pl.CostEstimate(flops=1, bytes_accessed=1, transcendentals=0)


class Pinned:
    def __init__(self, value, before):
        self.value, self.before = value, before
        self.shape, self.dtype = value.shape, value.dtype


def pin(value, *before):
    if isinstance(value, Pinned):
        return Pinned(value.value, (*value.before, *before))
    return Pinned(value, before)


def unpin(operands):
    arrays, before = [], []
    for one in operands:
        if isinstance(one, Pinned):
            before += [other for other in one.before if all(other is not had for had in before)]
            one = one.value
        arrays.append(one)
    return arrays, before


def call_kernel(kernel, grid_spec, out_shape, operands, scalars=0, aliases=()):
    arrays, before = unpin(operands)
    count, spare = len(arrays), len(before)

    def body(*refs):
        kernel(*refs[:count], *refs[count + spare :])

    spec = pltpu.PrefetchScalarGridSpec(
        num_scalar_prefetch=scalars,
        grid=grid_spec["grid"],
        in_specs=list(grid_spec["in_specs"]) + [pl.BlockSpec(memory_space=pl.ANY)] * spare,
        out_specs=grid_spec["out_specs"],
        scratch_shapes=grid_spec.get("scratch", ()),
    )
    return pl.pallas_call(
        body,
        grid_spec=spec,
        out_shape=out_shape,
        input_output_aliases=dict(aliases),
        compiler_params=pltpu.CompilerParams(
            dimension_semantics=("arbitrary",) * len(grid_spec["grid"]),
            vmem_limit_bytes=VMEM_BYTES,
        ),
        cost_estimate=SMALL_COST,
    )(*arrays, *before)


def run_kernel(kernel, grid, in_specs, out_specs, out_shape, scratch=()):
    def call(*operands):
        spec = {"grid": grid, "in_specs": in_specs, "out_specs": out_specs, "scratch": scratch}
        return call_kernel(kernel, spec, out_shape, operands)

    return call


def hold_kernel(value_ref, out_ref):
    del value_ref, out_ref


def settle(value):
    if not isinstance(value, Pinned):
        return value
    anywhere = pl.BlockSpec(memory_space=pl.ANY)
    return call_kernel(
        hold_kernel,
        {"grid": (1,), "in_specs": [anywhere], "out_specs": anywhere},
        jax.ShapeDtypeStruct(value.shape, value.dtype),
        [value],
        aliases=((0, 0),),
    )


def weight_shape(weight):
    return (weight[0].shape[0] * 2, weight[0].shape[1])


def with_weights(weights, places, body, first_step, *refs):
    side_ref, refs = refs[0], list(refs[1:])
    scratch = refs[len(refs) - 2 * len(weights) :]
    refs = refs[: len(refs) - 2 * len(weights)]
    count = sum(len(weight) for weight in weights)
    held = refs[places : places + count]
    rest = refs[:places] + refs[places + count :]
    ways = lax.axis_size("fsdp")

    @pl.when(first_step())
    def _():
        copies = []
        for number, weight in enumerate(weights):
            rows = weight_shape(weight)[0] // ways
            block = 0
            for part in weight:
                ref = held.pop(0)
                for place in range(part.shape[0] // rows):
                    other, index = divmod(block, ways // 2)
                    row = pl.multiple_of((2 * index + (side_ref[0] ^ other)) * rows, rows)
                    copies.append(
                        pltpu.make_async_copy(
                            ref.at[pl.ds(place * rows, rows), :],
                            scratch[2 * number].at[pl.ds(row, rows), :],
                            scratch[2 * number + 1].at[block],
                        )
                    )
                    block += 1
        for copy in copies:
            copy.start()
        for copy in copies:
            copy.wait()

    body(*rest[:places], *scratch[0::2], *rest[places:])


def run_weights(body, grid, before, weights, after, out_specs, out_shape, scratch=()):
    side = my_bit("fsdp", 1).astype(jnp.int32).reshape((1,))
    spare = []
    for weight in weights:
        spare += [
            pltpu.VMEM(weight_shape(weight), BF16),
            pltpu.SemaphoreType.DMA((lax.axis_size("fsdp"),)),
        ]

    def first_step():
        first = pl.program_id(0) == 0
        for axis in range(1, len(grid)):
            first = first & (pl.program_id(axis) == 0)
        return first

    return run_kernel(
        functools.partial(with_weights, weights, len(before), body, first_step),
        grid,
        [pl.BlockSpec(memory_space=pltpu.SMEM)]
        + [spec for spec, _ in before]
        + [pl.BlockSpec(memory_space=pl.ANY)] * sum(len(weight) for weight in weights)
        + [spec for spec, _ in after],
        out_specs,
        out_shape,
        list(scratch) + spare,
    )(
        side,
        *[one for _, one in before],
        *[part for weight in weights for part in weight],
        *[one for _, one in after],
    )


def fixed(shape):
    return pl.BlockSpec(shape, lambda *_: (0,) * len(shape))


def by_rows(cols):
    return pl.BlockSpec((TILE, cols), lambda step: (step, 0))


def dot_plain(left, right):
    return jnp.dot(left, right, preferred_element_type=F32)


def qkv_kernel(rotated, x_ref, w_ref, cos_ref, sin_ref, out_ref):
    half = HD // 2
    cosine, sine = cos_ref[...], sin_ref[...]
    for head in range(w_ref.shape[1] // HD):
        here = slice(head * HD, (head + 1) * HD)
        lin = dot_plain(x_ref[...], w_ref[:, here])
        if head < rotated:
            first, second = lin[:, :half], lin[:, half:]
            out_ref[:, head * HD : head * HD + half] = (first * cosine - second * sine).astype(BF16)
            out_ref[:, head * HD + half : (head + 1) * HD] = (
                second * cosine + first * sine
            ).astype(BF16)
        else:
            out_ref[:, here] = lin.astype(BF16)


def project_qkv(attn_input, full_qkv, cosine_table, sine_table, rotated):
    rows, depth = attn_input.shape
    cols = weight_shape(full_qkv)[1]
    return run_weights(
        functools.partial(qkv_kernel, rotated),
        (rows // TILE,),
        [(by_rows(depth), attn_input)],
        [full_qkv],
        [(by_rows(HD // 2), cosine_table), (by_rows(HD // 2), sine_table)],
        by_rows(cols),
        jax.ShapeDtypeStruct((rows, cols), BF16),
    )


def soft_rows(query, keys, first_row, length):
    scores = dot_last(query, keys) * (HD**-0.5)
    rows = first_row + lax.broadcasted_iota(jnp.int32, scores.shape, 0)
    cols = lax.broadcasted_iota(jnp.int32, scores.shape, 1)
    scores = jnp.where((cols <= rows) & (cols < length), scores, MASKED)
    exponent = jnp.exp(scores - jnp.max(scores, axis=-1, keepdims=True))
    return exponent / jnp.sum(exponent, axis=-1, keepdims=True)


def attend_kernel(blocks, length_ref, q_ref, k_ref, v_ref, out_ref):
    for block in range(blocks):

        @pl.when(pl.program_id(1) == block)
        def _():
            width = (block + 1) * TILE
            probs = soft_rows(q_ref[...], k_ref[:width, :], block * TILE, length_ref[0])
            out_ref[...] = dot_plain(probs.astype(BF16), v_ref[:width, :]).astype(BF16)


def attend(qkv_rot, lengths, heads, heads_kv):
    rows = qkv_rot.shape[0]
    group = heads // heads_kv
    blocks = rows // TILE
    return run_kernel(
        functools.partial(attend_kernel, blocks),
        (heads, blocks),
        [
            pl.BlockSpec(memory_space=pltpu.SMEM),
            pl.BlockSpec((TILE, HD), lambda head, step: (step, head)),
            pl.BlockSpec((rows, HD), lambda head, step: (0, heads + head // group)),
            pl.BlockSpec((rows, HD), lambda head, step: (0, heads + heads_kv + head // group)),
        ],
        pl.BlockSpec((TILE, HD), lambda head, step: (step, head)),
        jax.ShapeDtypeStruct((rows, heads * HD), BF16),
    )(lengths, qkv_rot, qkv_rot, qkv_rot)


def attend_back_kernel(
    blocks, group, x_ref, w_ref, length_ref, q_ref, k_ref, v_ref, cos_ref, sin_ref,
    cos_all, sin_all, dq_ref, dk_ref, dv_ref, dk_sum, dv_sum,
):
    half = HD // 2
    step, member = pl.program_id(1), pl.program_id(2)

    @pl.when((step == 0) & (member == 0))
    def _():
        dk_sum[...] = jnp.zeros_like(dk_sum)
        dv_sum[...] = jnp.zeros_like(dv_sum)

    def unrotate(value, cosine, sine):
        first, second = value[:, :half], value[:, half:]
        return jnp.concatenate(
            [first * cosine + second * sine, second * cosine - first * sine], axis=1
        ).astype(BF16)

    for block in range(blocks):

        @pl.when(step == block)
        def _():
            width = (block + 1) * TILE
            query, keys, values = q_ref[...], k_ref[:width, :], v_ref[:width, :]
            here = pl.multiple_of((pl.program_id(0) * group + member) * HD, HD)
            grad = dot_plain(x_ref[...], w_ref[:, pl.ds(here, HD)]).astype(BF16)
            probs = soft_rows(query, keys, block * TILE, length_ref[0])
            prob_grad = dot_last(grad, values)
            delta = jnp.sum(probs * prob_grad, axis=-1, keepdims=True)
            score_grad = (probs * (prob_grad - delta) * (HD**-0.5)).astype(BF16)
            dq_ref[...] = unrotate(dot_plain(score_grad, keys), cos_ref[...], sin_ref[...])
            dk_sum[:width, :] += dot_rows(score_grad, query)
            dv_sum[:width, :] += dot_rows(probs.astype(BF16), grad)

    @pl.when((step == blocks - 1) & (member == group - 1))
    def _():
        dk_ref[...] = unrotate(dk_sum[...], cos_all[...], sin_all[...])
        dv_ref[...] = dv_sum[...].astype(BF16)


def attend_back(attn_grad_in, full_out, qkv_rot, lengths, cosine_table, sine_table, heads, heads_kv):
    rows, depth = attn_grad_in.shape
    group = heads // heads_kv
    blocks = rows // TILE
    half = HD // 2
    return run_weights(
        functools.partial(attend_back_kernel, blocks, group),
        (heads_kv, blocks, group),
        [(pl.BlockSpec((TILE, depth), lambda kv, step, one: (step, 0)), attn_grad_in)],
        [full_out],
        [
            (pl.BlockSpec(memory_space=pltpu.SMEM), lengths),
            (pl.BlockSpec((TILE, HD), lambda kv, step, one: (step, kv * group + one)), qkv_rot),
            (pl.BlockSpec((rows, HD), lambda kv, step, one: (0, heads + kv)), qkv_rot),
            (pl.BlockSpec((rows, HD), lambda kv, step, one: (0, heads + heads_kv + kv)), qkv_rot),
            (pl.BlockSpec((TILE, half), lambda kv, step, one: (step, 0)), cosine_table),
            (pl.BlockSpec((TILE, half), lambda kv, step, one: (step, 0)), sine_table),
            (fixed((rows, half)), cosine_table),
            (fixed((rows, half)), sine_table),
        ],
        [
            pl.BlockSpec((TILE, HD), lambda kv, step, one: (step, kv * group + one)),
            pl.BlockSpec((rows, HD), lambda kv, step, one: (0, kv)),
            pl.BlockSpec((rows, HD), lambda kv, step, one: (0, kv)),
        ],
        [
            jax.ShapeDtypeStruct((rows, heads * HD), BF16),
            jax.ShapeDtypeStruct((rows, heads_kv * HD), BF16),
            jax.ShapeDtypeStruct((rows, heads_kv * HD), BF16),
        ],
        [pltpu.VMEM((rows, HD), F32), pltpu.VMEM((rows, HD), F32)],
    )


def mlp_kernel(x_ref, gate_ref, up_ref, hidden_ref, up_part_ref, gate_part_ref):
    for start in range(0, gate_ref.shape[1], TILE):
        here = slice(start, start + TILE)
        gate = dot_plain(x_ref[...], gate_ref[:, here])
        up = dot_plain(x_ref[...], up_ref[:, here])
        sig = jax.nn.sigmoid(gate)
        act = gate * sig
        hidden_ref[:, here] = (act * up).astype(BF16)
        gate_part_ref[:, here] = (up * sig * (1.0 + gate * (1.0 - sig))).astype(BF16)
        up_part_ref[:, here] = act.astype(BF16)


def mlp_forward(block, full_gate, full_up):
    rows, depth = block.shape
    cols = weight_shape(full_gate)[1]
    return run_weights(
        mlp_kernel,
        (rows // TILE,),
        [(by_rows(depth), block)],
        [full_gate, full_up],
        [],
        [by_rows(cols)] * 3,
        [jax.ShapeDtypeStruct((rows, cols), BF16)] * 3,
    )


def mlp_grad_kernel(x_ref, down_ref, up_part_ref, gate_part_ref, gate_ref, up_ref):
    for start in range(0, down_ref.shape[1], TILE):
        here = slice(start, start + TILE)
        hidden_grad = dot_plain(x_ref[...], down_ref[:, here])
        gate_ref[:, here] = (hidden_grad * gate_part_ref[:, here].astype(F32)).astype(BF16)
        up_ref[:, here] = (hidden_grad * up_part_ref[:, here].astype(F32)).astype(BF16)


def mlp_backward(block, full_down, up_part, gate_part):
    rows, depth = block.shape
    cols = weight_shape(full_down)[1]
    return run_weights(
        mlp_grad_kernel,
        (rows // TILE,),
        [(by_rows(depth), block)],
        [full_down],
        [(by_rows(cols), up_part), (by_rows(cols), gate_part)],
        [by_rows(cols)] * 2,
        [jax.ShapeDtypeStruct((rows, cols), BF16)] * 2,
    )


def back_kernel(count, tiles, *refs):
    lefts, rights, outs = refs[:count], refs[count : 2 * count], refs[2 * count :]

    def write(out_ref):
        for start in range(0, out_ref.shape[1], TILE):
            here = slice(start, start + TILE)
            total = dot_last(lefts[0][...], rights[0][here, :])
            for number in range(1, count):
                total += dot_last(lefts[number][...], rights[number][here, :])
            out_ref[:, here] = total.astype(BF16)

    for number in range(len(outs)):
        first, last = number * tiles, (number + 1) * tiles

        @pl.when((pl.program_id(0) >= first) & (pl.program_id(0) < last))
        def _(number=number):
            write(outs[number])


def back_product(*operands, parts=1):
    count = len(operands) // 2
    lefts, rights = operands[:count], operands[count:]
    rows = lefts[0].shape[0]
    cols = weight_shape(rights[0])[0]
    tiles = rows // TILE // parts
    return run_weights(
        functools.partial(back_kernel, count, tiles),
        (rows // TILE,),
        [(by_rows(left.shape[1]), left) for left in lefts],
        list(rights),
        [],
        [
            pl.BlockSpec(
                (TILE, cols), lambda step, part=part: (jnp.clip(step - part * tiles, 0, tiles - 1), 0)
            )
            for part in range(parts)
        ],
        [jax.ShapeDtypeStruct((rows // parts, cols), BF16)] * parts,
    )


def arrange_kernel(parts, place_ref, *refs):
    for number in range(parts):

        @pl.when(pl.program_id(0) == number)
        def _():
            refs[parts][...] = refs[number][...]


def arrange(parts, places):
    rows, width = parts[0].shape
    count = len(parts)
    place = {
        "grid": (count,),
        "in_specs": [pl.BlockSpec((rows, width), lambda step, place: (0, 0))] * count,
        "out_specs": pl.BlockSpec((rows, width), lambda step, place: (place[step], 0)),
    }
    return call_kernel(
        functools.partial(arrange_kernel, count),
        place,
        jax.ShapeDtypeStruct((rows * count, width), parts[0].dtype),
        [jnp.stack([jnp.asarray(one, jnp.int32) for one in places]), *parts],
        scalars=1,
    )


def rowwise_kernel(fn, operands, outs, *refs):
    results = fn(*[ref[...] for ref in refs[:operands]])
    targets = refs[operands:]
    for number in range(outs):
        targets[number][...] = results[number].astype(targets[number].dtype)
    for number in range(outs, len(targets)):
        partial = jnp.broadcast_to(
            jnp.sum(results[number], axis=0, keepdims=True), targets[number].shape
        )

        @pl.when(pl.program_id(0) == 0)
        def _(number=number, partial=partial):
            targets[number][...] = partial

        @pl.when(pl.program_id(0) > 0)
        def _(number=number, partial=partial):
            targets[number][...] += partial


def rowwise(fn, rows, operands, outs, sums=0):
    tile = rows // 4
    specs = []
    for array, first in operands:
        cols = array.shape[1]
        if first is None:
            specs.append(fixed(array.shape))
        else:
            specs.append(pl.BlockSpec((tile, cols), lambda step, at=first // tile: (step + at, 0)))
    cols = operands[0][0].shape[1]
    return run_kernel(
        functools.partial(rowwise_kernel, fn, len(operands), len(outs)),
        (4,),
        specs,
        [pl.BlockSpec((tile, cols), lambda step: (step, 0))] * len(outs) + [fixed((8, cols))] * sums,
        [jax.ShapeDtypeStruct((rows, cols), one) for one in outs]
        + [jax.ShapeDtypeStruct((8, cols), F32)] * sums,
    )(*[array for array, _ in operands])


def sum_tiles(*tiles):
    total = tiles[0].astype(F32)
    for tile in tiles[1:]:
        total = total + tile.astype(F32)
    return total


def add_low(rows, *operands):
    return rowwise(lambda *tiles: (sum_tiles(*tiles),), rows, operands, [BF16])[0]


def row_scale_of(values):
    return lax.rsqrt(jnp.mean(values * values, axis=-1, keepdims=True) + EPS_NORM)


def enter_norm(tokens, gain):
    def body(values, gain):
        values = values.astype(F32)
        return (values * row_scale_of(values) * gain,)

    return rowwise(body, tokens.shape[0], [(tokens, 0), (gain, None)], [BF16])[0]


def middle_norm(rows, operands, gain):
    def body(*tiles):
        values = sum_tiles(*tiles[:-1])
        return values, values * row_scale_of(values) * tiles[-1]

    return rowwise(body, rows, [*operands, (gain, None)], [F32, BF16])


def leave_norm(rows, operands, values, passed, gain, outs):
    def body(*tiles):
        incoming = sum_tiles(*tiles[:-3])
        values, passed, gain = tiles[-3].astype(F32), tiles[-2].astype(F32), tiles[-1]
        scale = row_scale_of(values)
        weighted = incoming * gain
        mean = jnp.mean(weighted * values, axis=-1, keepdims=True)
        result = passed + scale * weighted - values * scale**3 * mean
        return *[result for _ in outs], incoming * values * scale

    return rowwise(body, rows, [*operands, (values, 0), (passed, 0), (gain, None)], outs, 1)


def spread_kernel(count, groups, *refs):
    weights, out_ref = refs[:count], refs[-1]
    if groups == 1:
        start = 0
        for weight in weights:
            width = weight.shape[1]
            out_ref[:, start : start + width] = weight[...].astype(BF16)
            start += width
    else:
        width = out_ref.shape[1]
        for group in range(groups):

            @pl.when(lax.rem(pl.program_id(0), groups) == group)
            def _():
                here = slice(group * width, (group + 1) * width)
                out_ref[...] = weights[0][:, here].astype(BF16)


def spread(weights, groups):
    ways = lax.axis_size("fsdp") // 2
    rows = weights[0].shape[0]
    width = sum(weight.shape[1] for weight in weights) // groups
    return run_kernel(
        functools.partial(spread_kernel, len(weights), groups),
        (ways,),
        [fixed(weight.shape) for weight in weights],
        by_rows(width) if rows == TILE else pl.BlockSpec((rows, width), lambda step: (step, 0)),
        jax.ShapeDtypeStruct((ways * rows, width), BF16),
    )(*weights)


def weight_kernel(count, half, order_ref, *refs):
    lefts, rights = refs[:count], refs[count : 2 * count]
    sent_ref, kept_ref = refs[2 * count :]

    def write(out_ref):
        for start in range(0, out_ref.shape[1], TILE):
            here = slice(start, start + TILE)
            total = dot_rows(lefts[0][...], rights[0][:, here])
            for number in range(1, count):
                total += dot_rows(lefts[number][...], rights[number][:, here])
            out_ref[:, here] = total.astype(BF16)

    @pl.when(pl.program_id(0) < half)
    def _():
        write(sent_ref)

    @pl.when(pl.program_id(0) >= half)
    def _():
        write(kept_ref)


def weight_grad(lefts, rights):
    count = len(lefts)
    rows, depth = lefts[0].shape
    cols = rights[0].shape[1]
    ways = lax.axis_size("fsdp")
    block, half = depth // ways, ways // 2
    side = my_bit("fsdp", 1).astype(jnp.int32)
    pairs = 2 * jnp.arange(half, dtype=jnp.int32)
    order = jnp.concatenate([pairs + 1 - side, pairs + side])
    if block % 128:
        lefts = [settle(left) for left in lefts]
        rights = [settle(right) for right in rights]
        total = sum(dot_rows(left, right) for left, right in zip(lefts, rights))
        blocks = total.astype(BF16).reshape(ways, block, cols)[order].reshape(-1, cols)
        return blocks[: block * half], blocks[block * half :]
    place = {
        "grid": (ways,),
        "in_specs": [pl.BlockSpec((rows, block), lambda step, order: (0, order[step]))] * count
        + [pl.BlockSpec((rows, cols), lambda step, order: (0, 0))] * count,
        "out_specs": [
            pl.BlockSpec((block, cols), lambda step, order: (jnp.minimum(step, half - 1), 0)),
            pl.BlockSpec((block, cols), lambda step, order: (jnp.maximum(step - half, 0), 0)),
        ],
    }
    return call_kernel(
        functools.partial(weight_kernel, count, half),
        place,
        [jax.ShapeDtypeStruct((half * block, cols), BF16)] * 2,
        [order, *lefts, *rights],
        scalars=1,
    )


def finish_kernel(rows, groups, in_ref, out_ref, square_ref):
    width = in_ref.shape[1]
    total_square = jnp.zeros((1, 1), F32)
    for group in range(groups):
        total = jnp.zeros((rows, width), F32)
        for block in range(group, in_ref.shape[0] // rows, groups):
            total += in_ref[block * rows : (block + 1) * rows, :].astype(F32)
        out_ref[:, group * width : (group + 1) * width] = total
        total_square += jnp.sum(total * total)
    square_ref[...] = jnp.broadcast_to(total_square, square_ref.shape)


def finish_shard(arrived, rows, groups):
    width = arrived.shape[1]
    shard, square = run_kernel(
        functools.partial(finish_kernel, rows, groups),
        (1,),
        [fixed(arrived.shape)],
        [fixed((rows, width * groups)), fixed((8, 128))],
        [
            jax.ShapeDtypeStruct((rows, width * groups), F32),
            jax.ShapeDtypeStruct((8, 128), F32),
        ],
    )(arrived)
    return shard, square


AXES = ("fsdp", "tp")
PAIR = 2


def swap(value, fsdp_mask, tp_mask, odd_masks=None):
    fsdp_ways, tp_ways = lax.axis_size("fsdp"), lax.axis_size("tp")
    pairs = []
    for row in range(fsdp_ways):
        for col in range(tp_ways):
            masks = (fsdp_mask, tp_mask)
            if odd_masks is not None and col & 1:
                masks = odd_masks
            pairs.append((row * tp_ways + col, (row ^ masks[0]) * tp_ways + (col ^ masks[1])))
    return lax.ppermute(settle(value), AXES, pairs)


def swap_bit(value, axis, bit):
    return swap(value, bit, 0) if axis == "fsdp" else swap(value, 0, bit)


def my_bit(axis, bit):
    return (lax.axis_index(axis) // bit) % 2


def bits_of(ways):
    return [1 << power for power in reversed(range(ways.bit_length() - 1))]


def trade_far(blocks):
    ways = lax.axis_size("fsdp")
    groups = [list(range(side, ways, 2)) for side in range(2)]
    return lax.all_to_all(settle(blocks), "fsdp", 0, 0, axis_index_groups=groups, tiled=True)


def cross(value):
    return swap(value, 1, 0)


def swap_one(value):
    return swap(value, 0, 2, (PAIR, 0))


def swap_two(value):
    return swap(value, PAIR, 0, (0, 2))


def gather_slot(block, other):
    other = settle(other)
    me = lax.axis_index("tp")
    near, far = swap(block, 0, 1), swap(other, 0, 1)
    return arrange([block, other, near, far], [me, me ^ 2, me ^ 1, me ^ 3])


def slot_kernel(x_ref, w_ref, order_ref, *outs):
    rows = outs[0].shape[0]
    place = order_ref[pl.program_id(0)]
    left = x_ref[pl.ds(pl.multiple_of(place * rows, rows), rows), :]
    for number, out_ref in enumerate(outs):

        @pl.when(pl.program_id(0) == number)
        def _(out_ref=out_ref):
            for start in range(0, out_ref.shape[1], TILE):
                here = slice(start, start + TILE)
                out_ref[:, here] = dot_last(left, w_ref[here, :]).astype(BF16)


def slot_product(left, weight):
    me = lax.axis_index("tp")
    rows = left.shape[0] // 4
    cols = weight_shape(weight)[0]
    order = jnp.stack([me ^ 3, me ^ 1, me ^ 2, me]).astype(jnp.int32)
    return run_weights(
        slot_kernel,
        (4,),
        [(fixed(left.shape), left)],
        [weight],
        [(pl.BlockSpec(memory_space=pltpu.SMEM), order)],
        [fixed((rows, cols))] * 4,
        [jax.ShapeDtypeStruct((rows, cols), BF16)] * 4,
    )


def sum_everywhere(value):
    for bit in bits_of(lax.axis_size("tp"))[::-1]:
        value = value + swap(value, 0, bit)
    for bit in bits_of(lax.axis_size("fsdp")):
        value = value + swap(value, bit, 0)
    return value


def on_device(
    tokens,
    out_grad,
    lengths,
    w_query,
    w_key,
    w_value,
    w_out,
    w_gate,
    w_up,
    w_down,
    norm_attn,
    norm_mlp,
    moment_query,
    moment_key,
    moment_value,
    moment_out,
    moment_gate,
    moment_up,
    moment_down,
    moment_norm_attn,
    moment_norm_mlp,
    square_query,
    square_key,
    square_value,
    square_out,
    square_gate,
    square_up,
    square_down,
    square_norm_attn,
    square_norm_mlp,
):
    rows_dev = tokens.shape[0]
    tp_ways = lax.axis_size("tp")
    slot_rows = rows_dev * tp_ways
    heads, heads_kv = w_query.shape[1] // HD, w_key.shape[1] // HD
    shard_rows = w_query.shape[0]
    length = lengths[0]
    row_pos = lax.axis_index("tp") * rows_dev + jnp.arange(rows_dev)
    gain_attn, gain_mlp = norm_attn[None], norm_mlp[None]
    far_rows = shard_rows * (lax.axis_size("fsdp") // 2)

    normed_attn = enter_norm(tokens, gain_attn)
    slot_other = swap(normed_attn, 0, 2)
    qkv_blocks = spread([pin(w_query, normed_attn), w_key, w_value], 1)
    qkv_rows = trade_far(qkv_blocks)
    out_blocks = spread([pin(w_out, qkv_blocks)], 1)
    gate_blocks = spread([pin(w_gate, out_blocks)], 2)
    cosine_table, sine_table = rotary_tables(slot_rows, HD)
    full_qkv = (qkv_rows, cross(qkv_rows))
    cotangent = jnp.where(row_pos[:, None] < length, out_grad, jnp.zeros_like(out_grad))
    grad_pair = swap(cotangent, PAIR, 0)
    attn_input = gather_slot(normed_attn, pin(slot_other, grad_pair))
    out_rows = trade_far(pin(out_blocks, qkv_rows, attn_input))
    full_out = (out_rows, cross(out_rows))
    grad_other, grad_both = swap(cotangent, 0, 2), swap(grad_pair, 0, 2)
    gate_rows = trade_far(pin(gate_blocks, out_rows))

    qkv_rot = project_qkv(pin(attn_input, out_rows), full_qkv, cosine_table, sine_table, heads + heads_kv)
    odd = my_bit("tp", 1)
    grad_mine = arrange(
        [pin(cotangent, qkv_rot), grad_other, grad_pair, grad_both], [0, 1 + odd, 2 - odd, 3]
    )
    grad_near = swap(grad_mine, 0, 1)
    up_blocks = spread([pin(w_up, qkv_rot)], 2)
    attn_bf = attend(pin(qkv_rot, up_blocks), lengths, heads, heads_kv)
    attn_parts = slot_product(pin(attn_bf, grad_mine), full_out)
    attn_got = [swap(part, 0, 1) for part in attn_parts[:2]]
    attn_sent = add_low(rows_dev, (attn_parts[2], 0), (attn_got[0], 0))
    attn_last = swap(attn_sent, 0, 2)
    gate_rows = settle(pin(gate_rows, attn_sent))
    gate_crossed = cross(gate_rows)
    full_gate = (gate_rows, gate_crossed)
    up_rows = trade_far(pin(up_blocks, gate_rows))
    down_blocks = spread([pin(w_down, attn_sent)], 2)
    middle, normed_mlp = middle_norm(
        rows_dev,
        [
            (tokens, 0),
            (attn_parts[3], 0),
            (attn_got[1], 0),
            (pin(attn_last, down_blocks, grad_near), 0),
        ],
        gain_mlp,
    )
    first = swap_one(normed_mlp)
    second = swap_two(normed_mlp)
    up_rows = settle(pin(up_rows, first, gate_crossed))
    up_crossed = cross(up_rows)
    full_up = (up_rows, up_crossed)
    both = swap_two(first)
    mlp_mine = arrange([normed_mlp, first, second, pin(both, up_crossed)], range(4))
    mlp_near = arrange([swap(one, 0, 1) for one in (normed_mlp, first, second, both)], range(4))
    down_rows = trade_far(pin(down_blocks, up_rows, first))
    hid_mine, upp_mine, gatep_mine = mlp_forward(mlp_mine, full_gate, full_up)
    down_rows = settle(pin(down_rows, hid_mine))
    full_down = (down_rows, cross(down_rows))
    hid_near, upp_near, gatep_near = mlp_forward(pin(mlp_near, down_rows), full_gate, full_up)

    down_sent, down_own = weight_grad([grad_mine, grad_near], [hid_mine, hid_near])
    down_got = cross(down_sent)
    dgate_near, dup_near = mlp_backward(pin(grad_near, down_own), full_down, upp_near, gatep_near)
    dgate_mine, dup_mine = mlp_backward(
        pin(grad_mine, dgate_near), full_down, upp_mine, gatep_mine
    )
    gate_sent, gate_own = weight_grad([mlp_mine, mlp_near], [dgate_mine, dgate_near])
    gate_got = cross(gate_sent)
    up_sent, up_own = weight_grad([pin(mlp_mine, gate_own), mlp_near], [dup_mine, dup_near])
    up_got = cross(up_sent)
    down_far = trade_far(add_low(far_rows, (pin(down_got, gate_own), 0), (down_own, 0)))
    back_near = back_product(pin(dgate_near, up_own), dup_near, full_gate, full_up, parts=4)
    back_got = [swap(part, 0, 1) for part in back_near]
    back_mine = back_product(pin(dgate_mine, back_near[0], gate_got), dup_mine, full_gate, full_up, parts=4)
    sent = [add_low(rows_dev, (back_mine[one], 0), (back_got[one], 0)) for one in (2, 3)]
    back_two = [swap_two(one) for one in sent]
    (out_near,) = back_product(pin(hid_near, *sent), full_down)
    (out_mine,) = back_product(pin(hid_mine, out_near), full_down)
    sent = add_low(
        rows_dev, (back_mine[1], 0), (back_got[1], 0), (pin(back_two[1], out_mine, down_far), 0)
    )
    back_one = swap_one(sent)
    out_got = swap(pin(out_near, sent), 0, 1)
    gate_far = trade_far(add_low(far_rows, (pin(gate_got, sent), 0), (gate_own, 0)))
    middle_grad, low_grad, gain_mlp_part = leave_norm(
        rows_dev,
        [(back_mine[0], 0), (back_got[0], 0), (back_two[0], 0), (pin(back_one, up_got), 0)],
        middle,
        cotangent,
        gain_mlp,
        [F32, BF16],
    )
    slot_other = swap(low_grad, 0, 2)
    attn_grad_in = gather_slot(low_grad, slot_other)
    proj_sent, proj_own = weight_grad([attn_grad_in], [attn_bf])
    proj_got = cross(proj_sent)
    query_grad, key_grad, value_grad = attend_back(
        pin(attn_grad_in, proj_own, gate_far),
        full_out, qkv_rot, lengths, cosine_table, sine_table, heads, heads_kv,
    )
    up_far = trade_far(add_low(far_rows, (pin(up_got, attn_grad_in, gate_far), 0), (up_own, 0)))
    shard_down, square_down_part = finish_shard(pin(down_far, query_grad), shard_rows, 2)
    sent = add_low(
        2 * rows_dev, (out_mine, 2 * rows_dev), (pin(out_got, query_grad), 2 * rows_dev)
    )
    out_two = swap_two(sent)
    qkv_grad = jnp.concatenate([query_grad, key_grad, value_grad], axis=1)
    qkv_sent, qkv_own = weight_grad([attn_input], [qkv_grad])
    qkv_got = cross(qkv_sent)
    input_parts = slot_product(pin(qkv_grad, qkv_own, proj_got), full_qkv)
    input_got = [swap(part, 0, 1) for part in input_parts[:2]]
    proj_low = add_low(far_rows, (pin(proj_got, up_far, input_parts[3]), 0), (proj_own, 0))
    proj_far = trade_far(proj_low)
    sent = add_low(
        rows_dev, (out_mine, rows_dev), (out_got, rows_dev), (pin(out_two, proj_low), rows_dev)
    )
    out_one = swap_one(sent)
    input_sent = add_low(
        rows_dev, (input_parts[2], 0), (pin(input_got[0], sent, qkv_got), 0)
    )
    input_last = swap(input_sent, 0, 2)
    shard_gate, square_gate_part = finish_shard(pin(gate_far, input_sent), shard_rows, 2)
    shard_up, square_up_part = finish_shard(pin(up_far, input_sent), shard_rows, 2)
    qkv_far = trade_far(add_low(far_rows, (pin(qkv_got, proj_far), 0), (qkv_own, 0)))
    input_grad, gain_attn_part = leave_norm(
        rows_dev,
        [(input_parts[3], 0), (input_got[1], 0), (pin(input_last, shard_gate, shard_up), 0)],
        tokens,
        middle_grad,
        gain_attn,
        [F32],
    )
    block_out = add_low(
        rows_dev,
        (middle, 0),
        (out_mine, 0),
        (out_got, 0),
        (out_two, 0),
        (pin(out_one, input_grad), 0),
    )
    gains = jnp.concatenate([gain_attn_part[0], gain_mlp_part[0]]).reshape(-1, 128)
    gains = sum_everywhere(gains).reshape(-1)
    shard_out, square_out_part = finish_shard(proj_far, shard_rows, 1)
    shard_qkv, square_qkv_part = finish_shard(qkv_far, shard_rows, 1)
    width_query, width_key = w_query.shape[1], w_key.shape[1]
    shard_grads = (
        shard_qkv[:, :width_query],
        shard_qkv[:, width_query : width_query + width_key],
        shard_qkv[:, width_query + width_key :],
        shard_out,
        shard_gate,
        shard_up,
        shard_down,
    )
    square_part = (
        square_down_part + square_gate_part + square_up_part + square_qkv_part + square_out_part
    )
    square_total = sum_everywhere(square_part)[0, 0]
    gain_attn_grad = gains[: norm_attn.shape[0]]
    gain_mlp_grad = gains[norm_attn.shape[0] :]
    clip_norm = jnp.sqrt(
        square_total
        + jnp.sum(gain_attn_grad * gain_attn_grad)
        + jnp.sum(gain_mlp_grad * gain_mlp_grad)
    )
    factor = jnp.minimum(1.0, MAX_NORM / (clip_norm + 1e-06))
    every_grad = tuple(shard_grads) + (gain_attn_grad, gain_mlp_grad)
    params = (w_query, w_key, w_value, w_out, w_gate, w_up, w_down, norm_attn, norm_mlp)
    moments = (
        moment_query,
        moment_key,
        moment_value,
        moment_out,
        moment_gate,
        moment_up,
        moment_down,
        moment_norm_attn,
        moment_norm_mlp,
    )
    squares = (
        square_query,
        square_key,
        square_value,
        square_out,
        square_gate,
        square_up,
        square_down,
        square_norm_attn,
        square_norm_mlp,
    )
    results = [
        adam_step(params[number], every_grad[number], moments[number], squares[number], factor)
        for number in range(9)
    ]
    return (
        block_out,
        input_grad,
        every_grad[0],
        every_grad[1],
        every_grad[2],
        every_grad[3],
        every_grad[4],
        every_grad[5],
        every_grad[6],
        every_grad[7],
        every_grad[8],
        results[0][0],
        results[1][0],
        results[2][0],
        results[3][0],
        results[4][0],
        results[5][0],
        results[6][0],
        results[7][0],
        results[8][0],
        results[0][1],
        results[1][1],
        results[2][1],
        results[3][1],
        results[4][1],
        results[5][1],
        results[6][1],
        results[7][1],
        results[8][1],
        results[0][2],
        results[1][2],
        results[2][2],
        results[3][2],
        results[4][2],
        results[5][2],
        results[6][2],
        results[7][2],
        results[8][2],
        clip_norm,
    )


def solution(mesh):
    return jax.shard_map(
        on_device,
        mesh=mesh,
        in_specs=(
            P(("fsdp", "tp"), None),
            P(("fsdp", "tp"), None),
            P("fsdp"),
            P("fsdp", "tp"),
            P("fsdp", "tp"),
            P("fsdp", "tp"),
            P("fsdp", "tp"),
            P("fsdp", "tp"),
            P("fsdp", "tp"),
            P("fsdp", "tp"),
            P(),
            P(),
            P("fsdp", "tp"),
            P("fsdp", "tp"),
            P("fsdp", "tp"),
            P("fsdp", "tp"),
            P("fsdp", "tp"),
            P("fsdp", "tp"),
            P("fsdp", "tp"),
            P(),
            P(),
            P("fsdp", "tp"),
            P("fsdp", "tp"),
            P("fsdp", "tp"),
            P("fsdp", "tp"),
            P("fsdp", "tp"),
            P("fsdp", "tp"),
            P("fsdp", "tp"),
            P(),
            P(),
        ),
        out_specs=(
            P(("fsdp", "tp"), None),
            P(("fsdp", "tp"), None),
            P("fsdp", "tp"),
            P("fsdp", "tp"),
            P("fsdp", "tp"),
            P("fsdp", "tp"),
            P("fsdp", "tp"),
            P("fsdp", "tp"),
            P("fsdp", "tp"),
            P(),
            P(),
            P("fsdp", "tp"),
            P("fsdp", "tp"),
            P("fsdp", "tp"),
            P("fsdp", "tp"),
            P("fsdp", "tp"),
            P("fsdp", "tp"),
            P("fsdp", "tp"),
            P(),
            P(),
            P("fsdp", "tp"),
            P("fsdp", "tp"),
            P("fsdp", "tp"),
            P("fsdp", "tp"),
            P("fsdp", "tp"),
            P("fsdp", "tp"),
            P("fsdp", "tp"),
            P(),
            P(),
            P("fsdp", "tp"),
            P("fsdp", "tp"),
            P("fsdp", "tp"),
            P("fsdp", "tp"),
            P("fsdp", "tp"),
            P("fsdp", "tp"),
            P("fsdp", "tp"),
            P(),
            P(),
            P(),
        ),
        check_vma=False,
    )
```

```python
import functools

import jax
import jax.numpy as jnp
from jax import lax
from jax.experimental import pallas as pl
from jax.experimental.pallas import tpu as pltpu
from jax.sharding import PartitionSpec as P

HD = 256
STEP = 10


EPS_NORM = 1e-05
THETA = 1000042.0
LEARN_RATE = 0.02
BETA_ONE = 0.9
BETA_TWO = 0.95
ADAM_EPS = 1e-08
WEIGHT_DECAY = 0.1
MAX_NORM = 1.0
MASKED = -1000000000.0


def rotary_tables(count, head_dim):
    positions = jnp.arange(count).astype(jnp.float32)
    inverse = THETA ** (-2.0 * jnp.arange(head_dim // 2).astype(jnp.float32) / head_dim)
    angles = positions[:, None] * inverse[None, :]
    return (jnp.cos(angles), jnp.sin(angles))


def dot_rows(left, right):
    return lax.dot_general(
        left, right, (((0,), (0,)), ((), ())), preferred_element_type=jnp.float32
    )


def dot_last(left, right):
    return lax.dot_general(
        left, right, (((1,), (1,)), ((), ())), preferred_element_type=jnp.float32
    )


def adam_step(master, gradient, moment, square, factor):
    clipped = gradient * factor
    new_moment = BETA_ONE * moment + (1.0 - BETA_ONE) * clipped
    new_square = BETA_TWO * square + (1.0 - BETA_TWO) * clipped * clipped
    moment_hat = new_moment / (1.0 - BETA_ONE**STEP)
    square_hat = new_square / (1.0 - BETA_TWO**STEP)
    update = -LEARN_RATE * (moment_hat / (jnp.sqrt(square_hat) + ADAM_EPS) + WEIGHT_DECAY * master)
    return (new_moment, new_square, update)


F32, BF16 = jnp.float32, jnp.bfloat16
TILE = 256
VMEM_BYTES = 48 * 1024 * 1024
SMALL_COST = pl.CostEstimate(flops=1, bytes_accessed=1, transcendentals=0)


class Pinned:
    def __init__(self, value, before):
        self.value, self.before = value, before
        self.shape, self.dtype = value.shape, value.dtype


def pin(value, *before):
    if isinstance(value, Pinned):
        return Pinned(value.value, (*value.before, *before))
    return Pinned(value, before)


def unpin(operands):
    arrays, before = [], []
    for one in operands:
        if isinstance(one, Pinned):
            before += [other for other in one.before if all(other is not had for had in before)]
            one = one.value
        arrays.append(one)
    return arrays, before


def call_kernel(kernel, grid_spec, out_shape, operands, scalars=0, aliases=()):
    arrays, before = unpin(operands)
    count, spare = len(arrays), len(before)

    def body(*refs):
        kernel(*refs[:count], *refs[count + spare :])

    spec = pltpu.PrefetchScalarGridSpec(
        num_scalar_prefetch=scalars,
        grid=grid_spec["grid"],
        in_specs=list(grid_spec["in_specs"]) + [pl.BlockSpec(memory_space=pl.ANY)] * spare,
        out_specs=grid_spec["out_specs"],
        scratch_shapes=grid_spec.get("scratch", ()),
    )
    return pl.pallas_call(
        body,
        grid_spec=spec,
        out_shape=out_shape,
        input_output_aliases=dict(aliases),
        compiler_params=pltpu.CompilerParams(
            dimension_semantics=("arbitrary",) * len(grid_spec["grid"]),
            vmem_limit_bytes=VMEM_BYTES,
        ),
        cost_estimate=SMALL_COST,
    )(*arrays, *before)


def run_kernel(kernel, grid, in_specs, out_specs, out_shape, scratch=()):
    def call(*operands):
        spec = {"grid": grid, "in_specs": in_specs, "out_specs": out_specs, "scratch": scratch}
        return call_kernel(kernel, spec, out_shape, operands)

    return call


def hold_kernel(value_ref, out_ref):
    del value_ref, out_ref


def settle(value):
    if not isinstance(value, Pinned):
        return value
    anywhere = pl.BlockSpec(memory_space=pl.ANY)
    return call_kernel(
        hold_kernel,
        {"grid": (1,), "in_specs": [anywhere], "out_specs": anywhere},
        jax.ShapeDtypeStruct(value.shape, value.dtype),
        [value],
        aliases=((0, 0),),
    )


def weight_shape(weight):
    return (weight[0].shape[0] * 2, weight[0].shape[1])


def with_weights(weights, places, body, first_step, *refs):
    side_ref, refs = refs[0], list(refs[1:])
    scratch = refs[len(refs) - 2 * len(weights) :]
    refs = refs[: len(refs) - 2 * len(weights)]
    count = sum(len(weight) for weight in weights)
    held = refs[places : places + count]
    rest = refs[:places] + refs[places + count :]
    ways = lax.axis_size("fsdp")

    @pl.when(first_step())
    def _():
        copies = []
        for number, weight in enumerate(weights):
            rows = weight_shape(weight)[0] // ways
            block = 0
            for part in weight:
                ref = held.pop(0)
                for place in range(part.shape[0] // rows):
                    other, index = divmod(block, ways // 2)
                    row = pl.multiple_of((2 * index + (side_ref[0] ^ other)) * rows, rows)
                    copies.append(
                        pltpu.make_async_copy(
                            ref.at[pl.ds(place * rows, rows), :],
                            scratch[2 * number].at[pl.ds(row, rows), :],
                            scratch[2 * number + 1].at[block],
                        )
                    )
                    block += 1
        for copy in copies:
            copy.start()
        for copy in copies:
            copy.wait()

    body(*rest[:places], *scratch[0::2], *rest[places:])


def run_weights(body, grid, before, weights, after, out_specs, out_shape, scratch=()):
    side = my_bit("fsdp", 1).astype(jnp.int32).reshape((1,))
    spare = []
    for weight in weights:
        spare += [
            pltpu.VMEM(weight_shape(weight), BF16),
            pltpu.SemaphoreType.DMA((lax.axis_size("fsdp"),)),
        ]

    def first_step():
        first = pl.program_id(0) == 0
        for axis in range(1, len(grid)):
            first = first & (pl.program_id(axis) == 0)
        return first

    return run_kernel(
        functools.partial(with_weights, weights, len(before), body, first_step),
        grid,
        [pl.BlockSpec(memory_space=pltpu.SMEM)]
        + [spec for spec, _ in before]
        + [pl.BlockSpec(memory_space=pl.ANY)] * sum(len(weight) for weight in weights)
        + [spec for spec, _ in after],
        out_specs,
        out_shape,
        list(scratch) + spare,
    )(
        side,
        *[one for _, one in before],
        *[part for weight in weights for part in weight],
        *[one for _, one in after],
    )


def fixed(shape):
    return pl.BlockSpec(shape, lambda *_: (0,) * len(shape))


def by_rows(cols):
    return pl.BlockSpec((TILE, cols), lambda step: (step, 0))


def dot_plain(left, right):
    return jnp.dot(left, right, preferred_element_type=F32)


def qkv_kernel(rotated, x_ref, w_ref, cos_ref, sin_ref, out_ref):
    half = HD // 2
    cosine, sine = cos_ref[...], sin_ref[...]
    for head in range(w_ref.shape[1] // HD):
        here = slice(head * HD, (head + 1) * HD)
        lin = dot_plain(x_ref[...], w_ref[:, here])
        if head < rotated:
            first, second = lin[:, :half], lin[:, half:]
            out_ref[:, head * HD : head * HD + half] = (first * cosine - second * sine).astype(BF16)
            out_ref[:, head * HD + half : (head + 1) * HD] = (
                second * cosine + first * sine
            ).astype(BF16)
        else:
            out_ref[:, here] = lin.astype(BF16)


def project_qkv(attn_input, full_qkv, cosine_table, sine_table, rotated):
    rows, depth = attn_input.shape
    cols = weight_shape(full_qkv)[1]
    return run_weights(
        functools.partial(qkv_kernel, rotated),
        (rows // TILE,),
        [(by_rows(depth), attn_input)],
        [full_qkv],
        [(by_rows(HD // 2), cosine_table), (by_rows(HD // 2), sine_table)],
        by_rows(cols),
        jax.ShapeDtypeStruct((rows, cols), BF16),
    )


def soft_rows(query, keys, first_row, length):
    scores = dot_last(query, keys) * (HD**-0.5)
    rows = first_row + lax.broadcasted_iota(jnp.int32, scores.shape, 0)
    cols = lax.broadcasted_iota(jnp.int32, scores.shape, 1)
    scores = jnp.where((cols <= rows) & (cols < length), scores, MASKED)
    exponent = jnp.exp(scores - jnp.max(scores, axis=-1, keepdims=True))
    return exponent / jnp.sum(exponent, axis=-1, keepdims=True)


def attend_kernel(blocks, length_ref, q_ref, k_ref, v_ref, out_ref):
    for block in range(blocks):

        @pl.when(pl.program_id(1) == block)
        def _():
            width = (block + 1) * TILE
            probs = soft_rows(q_ref[...], k_ref[:width, :], block * TILE, length_ref[0])
            out_ref[...] = dot_plain(probs.astype(BF16), v_ref[:width, :]).astype(BF16)


def attend(qkv_rot, lengths, heads, heads_kv):
    rows = qkv_rot.shape[0]
    group = heads // heads_kv
    blocks = rows // TILE
    return run_kernel(
        functools.partial(attend_kernel, blocks),
        (heads, blocks),
        [
            pl.BlockSpec(memory_space=pltpu.SMEM),
            pl.BlockSpec((TILE, HD), lambda head, step: (step, head)),
            pl.BlockSpec((rows, HD), lambda head, step: (0, heads + head // group)),
            pl.BlockSpec((rows, HD), lambda head, step: (0, heads + heads_kv + head // group)),
        ],
        pl.BlockSpec((TILE, HD), lambda head, step: (step, head)),
        jax.ShapeDtypeStruct((rows, heads * HD), BF16),
    )(lengths, qkv_rot, qkv_rot, qkv_rot)


def attend_back_kernel(
    blocks, group, x_ref, w_ref, length_ref, q_ref, k_ref, v_ref, cos_ref, sin_ref,
    cos_all, sin_all, dq_ref, dk_ref, dv_ref, dk_sum, dv_sum,
):
    half = HD // 2
    step, member = pl.program_id(1), pl.program_id(2)

    @pl.when((step == 0) & (member == 0))
    def _():
        dk_sum[...] = jnp.zeros_like(dk_sum)
        dv_sum[...] = jnp.zeros_like(dv_sum)

    def unrotate(value, cosine, sine):
        first, second = value[:, :half], value[:, half:]
        return jnp.concatenate(
            [first * cosine + second * sine, second * cosine - first * sine], axis=1
        ).astype(BF16)

    for block in range(blocks):

        @pl.when(step == block)
        def _():
            width = (block + 1) * TILE
            query, keys, values = q_ref[...], k_ref[:width, :], v_ref[:width, :]
            here = pl.multiple_of((pl.program_id(0) * group + member) * HD, HD)
            grad = dot_plain(x_ref[...], w_ref[:, pl.ds(here, HD)]).astype(BF16)
            probs = soft_rows(query, keys, block * TILE, length_ref[0])
            prob_grad = dot_last(grad, values)
            delta = jnp.sum(probs * prob_grad, axis=-1, keepdims=True)
            score_grad = (probs * (prob_grad - delta) * (HD**-0.5)).astype(BF16)
            dq_ref[...] = unrotate(dot_plain(score_grad, keys), cos_ref[...], sin_ref[...])
            dk_sum[:width, :] += dot_rows(score_grad, query)
            dv_sum[:width, :] += dot_rows(probs.astype(BF16), grad)

    @pl.when((step == blocks - 1) & (member == group - 1))
    def _():
        dk_ref[...] = unrotate(dk_sum[...], cos_all[...], sin_all[...])
        dv_ref[...] = dv_sum[...].astype(BF16)


def attend_back(attn_grad_in, full_out, qkv_rot, lengths, cosine_table, sine_table, heads, heads_kv):
    rows, depth = attn_grad_in.shape
    group = heads // heads_kv
    blocks = rows // TILE
    half = HD // 2
    return run_weights(
        functools.partial(attend_back_kernel, blocks, group),
        (heads_kv, blocks, group),
        [(pl.BlockSpec((TILE, depth), lambda kv, step, one: (step, 0)), attn_grad_in)],
        [full_out],
        [
            (pl.BlockSpec(memory_space=pltpu.SMEM), lengths),
            (pl.BlockSpec((TILE, HD), lambda kv, step, one: (step, kv * group + one)), qkv_rot),
            (pl.BlockSpec((rows, HD), lambda kv, step, one: (0, heads + kv)), qkv_rot),
            (pl.BlockSpec((rows, HD), lambda kv, step, one: (0, heads + heads_kv + kv)), qkv_rot),
            (pl.BlockSpec((TILE, half), lambda kv, step, one: (step, 0)), cosine_table),
            (pl.BlockSpec((TILE, half), lambda kv, step, one: (step, 0)), sine_table),
            (fixed((rows, half)), cosine_table),
            (fixed((rows, half)), sine_table),
        ],
        [
            pl.BlockSpec((TILE, HD), lambda kv, step, one: (step, kv * group + one)),
            pl.BlockSpec((rows, HD), lambda kv, step, one: (0, kv)),
            pl.BlockSpec((rows, HD), lambda kv, step, one: (0, kv)),
        ],
        [
            jax.ShapeDtypeStruct((rows, heads * HD), BF16),
            jax.ShapeDtypeStruct((rows, heads_kv * HD), BF16),
            jax.ShapeDtypeStruct((rows, heads_kv * HD), BF16),
        ],
        [pltpu.VMEM((rows, HD), F32), pltpu.VMEM((rows, HD), F32)],
    )


def mlp_kernel(x_ref, gate_ref, up_ref, hidden_ref, up_part_ref, gate_part_ref):
    for start in range(0, gate_ref.shape[1], TILE):
        here = slice(start, start + TILE)
        gate = dot_plain(x_ref[...], gate_ref[:, here])
        up = dot_plain(x_ref[...], up_ref[:, here])
        sig = jax.nn.sigmoid(gate)
        act = gate * sig
        hidden_ref[:, here] = (act * up).astype(BF16)
        gate_part_ref[:, here] = (up * sig * (1.0 + gate * (1.0 - sig))).astype(BF16)
        up_part_ref[:, here] = act.astype(BF16)


def mlp_forward(block, full_gate, full_up):
    rows, depth = block.shape
    cols = weight_shape(full_gate)[1]
    return run_weights(
        mlp_kernel,
        (rows // TILE,),
        [(by_rows(depth), block)],
        [full_gate, full_up],
        [],
        [by_rows(cols)] * 3,
        [jax.ShapeDtypeStruct((rows, cols), BF16)] * 3,
    )


def mlp_grad_kernel(x_ref, down_ref, up_part_ref, gate_part_ref, gate_ref, up_ref):
    for start in range(0, down_ref.shape[1], TILE):
        here = slice(start, start + TILE)
        hidden_grad = dot_plain(x_ref[...], down_ref[:, here])
        gate_ref[:, here] = (hidden_grad * gate_part_ref[:, here].astype(F32)).astype(BF16)
        up_ref[:, here] = (hidden_grad * up_part_ref[:, here].astype(F32)).astype(BF16)


def mlp_backward(block, full_down, up_part, gate_part):
    rows, depth = block.shape
    cols = weight_shape(full_down)[1]
    return run_weights(
        mlp_grad_kernel,
        (rows // TILE,),
        [(by_rows(depth), block)],
        [full_down],
        [(by_rows(cols), up_part), (by_rows(cols), gate_part)],
        [by_rows(cols)] * 2,
        [jax.ShapeDtypeStruct((rows, cols), BF16)] * 2,
    )


def back_kernel(count, tiles, *refs):
    lefts, rights, outs = refs[:count], refs[count : 2 * count], refs[2 * count :]

    def write(out_ref):
        for start in range(0, out_ref.shape[1], TILE):
            here = slice(start, start + TILE)
            total = dot_last(lefts[0][...], rights[0][here, :])
            for number in range(1, count):
                total += dot_last(lefts[number][...], rights[number][here, :])
            out_ref[:, here] = total.astype(BF16)

    for number in range(len(outs)):
        first, last = number * tiles, (number + 1) * tiles

        @pl.when((pl.program_id(0) >= first) & (pl.program_id(0) < last))
        def _(number=number):
            write(outs[number])


def back_product(*operands, parts=1):
    count = len(operands) // 2
    lefts, rights = operands[:count], operands[count:]
    rows = lefts[0].shape[0]
    cols = weight_shape(rights[0])[0]
    tiles = rows // TILE // parts
    return run_weights(
        functools.partial(back_kernel, count, tiles),
        (rows // TILE,),
        [(by_rows(left.shape[1]), left) for left in lefts],
        list(rights),
        [],
        [
            pl.BlockSpec(
                (TILE, cols), lambda step, part=part: (jnp.clip(step - part * tiles, 0, tiles - 1), 0)
            )
            for part in range(parts)
        ],
        [jax.ShapeDtypeStruct((rows // parts, cols), BF16)] * parts,
    )


def arrange_kernel(parts, place_ref, *refs):
    for number in range(parts):

        @pl.when(pl.program_id(0) == number)
        def _():
            refs[parts][...] = refs[number][...]


def arrange(parts, places):
    rows, width = parts[0].shape
    count = len(parts)
    place = {
        "grid": (count,),
        "in_specs": [pl.BlockSpec((rows, width), lambda step, place: (0, 0))] * count,
        "out_specs": pl.BlockSpec((rows, width), lambda step, place: (place[step], 0)),
    }
    return call_kernel(
        functools.partial(arrange_kernel, count),
        place,
        jax.ShapeDtypeStruct((rows * count, width), parts[0].dtype),
        [jnp.stack([jnp.asarray(one, jnp.int32) for one in places]), *parts],
        scalars=1,
    )


def rowwise_kernel(fn, operands, outs, *refs):
    results = fn(*[ref[...] for ref in refs[:operands]])
    targets = refs[operands:]
    for number in range(outs):
        targets[number][...] = results[number].astype(targets[number].dtype)
    for number in range(outs, len(targets)):
        partial = jnp.broadcast_to(
            jnp.sum(results[number], axis=0, keepdims=True), targets[number].shape
        )

        @pl.when(pl.program_id(0) == 0)
        def _(number=number, partial=partial):
            targets[number][...] = partial

        @pl.when(pl.program_id(0) > 0)
        def _(number=number, partial=partial):
            targets[number][...] += partial


def rowwise(fn, rows, operands, outs, sums=0):
    tile = rows // 4
    specs = []
    for array, first in operands:
        cols = array.shape[1]
        if first is None:
            specs.append(fixed(array.shape))
        else:
            specs.append(pl.BlockSpec((tile, cols), lambda step, at=first // tile: (step + at, 0)))
    cols = operands[0][0].shape[1]
    return run_kernel(
        functools.partial(rowwise_kernel, fn, len(operands), len(outs)),
        (4,),
        specs,
        [pl.BlockSpec((tile, cols), lambda step: (step, 0))] * len(outs) + [fixed((8, cols))] * sums,
        [jax.ShapeDtypeStruct((rows, cols), one) for one in outs]
        + [jax.ShapeDtypeStruct((8, cols), F32)] * sums,
    )(*[array for array, _ in operands])


def sum_tiles(*tiles):
    total = tiles[0].astype(F32)
    for tile in tiles[1:]:
        total = total + tile.astype(F32)
    return total


def add_low(rows, *operands):
    return rowwise(lambda *tiles: (sum_tiles(*tiles),), rows, operands, [BF16])[0]


def row_scale_of(values):
    return lax.rsqrt(jnp.mean(values * values, axis=-1, keepdims=True) + EPS_NORM)


def enter_norm(tokens, gain):
    def body(values, gain):
        values = values.astype(F32)
        return (values * row_scale_of(values) * gain,)

    return rowwise(body, tokens.shape[0], [(tokens, 0), (gain, None)], [BF16])[0]


def middle_norm(rows, operands, gain):
    def body(*tiles):
        values = sum_tiles(*tiles[:-1])
        return values, values * row_scale_of(values) * tiles[-1]

    return rowwise(body, rows, [*operands, (gain, None)], [F32, BF16])


def leave_norm(rows, operands, values, passed, gain, outs):
    def body(*tiles):
        incoming = sum_tiles(*tiles[:-3])
        values, passed, gain = tiles[-3].astype(F32), tiles[-2].astype(F32), tiles[-1]
        scale = row_scale_of(values)
        weighted = incoming * gain
        mean = jnp.mean(weighted * values, axis=-1, keepdims=True)
        result = passed + scale * weighted - values * scale**3 * mean
        return *[result for _ in outs], incoming * values * scale

    return rowwise(body, rows, [*operands, (values, 0), (passed, 0), (gain, None)], outs, 1)


def spread_kernel(count, groups, *refs):
    weights, out_ref = refs[:count], refs[-1]
    if groups == 1:
        start = 0
        for weight in weights:
            width = weight.shape[1]
            out_ref[:, start : start + width] = weight[...].astype(BF16)
            start += width
    else:
        width = out_ref.shape[1]
        for group in range(groups):

            @pl.when(lax.rem(pl.program_id(0), groups) == group)
            def _():
                here = slice(group * width, (group + 1) * width)
                out_ref[...] = weights[0][:, here].astype(BF16)


def spread(weights, groups):
    ways = lax.axis_size("fsdp") // 2
    rows = weights[0].shape[0]
    width = sum(weight.shape[1] for weight in weights) // groups
    return run_kernel(
        functools.partial(spread_kernel, len(weights), groups),
        (ways,),
        [fixed(weight.shape) for weight in weights],
        by_rows(width) if rows == TILE else pl.BlockSpec((rows, width), lambda step: (step, 0)),
        jax.ShapeDtypeStruct((ways * rows, width), BF16),
    )(*weights)


def weight_kernel(count, half, order_ref, *refs):
    lefts, rights = refs[:count], refs[count : 2 * count]
    sent_ref, kept_ref = refs[2 * count :]

    def write(out_ref):
        for start in range(0, out_ref.shape[1], TILE):
            here = slice(start, start + TILE)
            total = dot_rows(lefts[0][...], rights[0][:, here])
            for number in range(1, count):
                total += dot_rows(lefts[number][...], rights[number][:, here])
            out_ref[:, here] = total.astype(BF16)

    @pl.when(pl.program_id(0) < half)
    def _():
        write(sent_ref)

    @pl.when(pl.program_id(0) >= half)
    def _():
        write(kept_ref)


def weight_grad(lefts, rights):
    count = len(lefts)
    rows, depth = lefts[0].shape
    cols = rights[0].shape[1]
    ways = lax.axis_size("fsdp")
    block, half = depth // ways, ways // 2
    side = my_bit("fsdp", 1).astype(jnp.int32)
    pairs = 2 * jnp.arange(half, dtype=jnp.int32)
    order = jnp.concatenate([pairs + 1 - side, pairs + side])
    if block % 128:
        lefts = [settle(left) for left in lefts]
        rights = [settle(right) for right in rights]
        total = sum(dot_rows(left, right) for left, right in zip(lefts, rights))
        blocks = total.astype(BF16).reshape(ways, block, cols)[order].reshape(-1, cols)
        return blocks[: block * half], blocks[block * half :]
    place = {
        "grid": (ways,),
        "in_specs": [pl.BlockSpec((rows, block), lambda step, order: (0, order[step]))] * count
        + [pl.BlockSpec((rows, cols), lambda step, order: (0, 0))] * count,
        "out_specs": [
            pl.BlockSpec((block, cols), lambda step, order: (jnp.minimum(step, half - 1), 0)),
            pl.BlockSpec((block, cols), lambda step, order: (jnp.maximum(step - half, 0), 0)),
        ],
    }
    return call_kernel(
        functools.partial(weight_kernel, count, half),
        place,
        [jax.ShapeDtypeStruct((half * block, cols), BF16)] * 2,
        [order, *lefts, *rights],
        scalars=1,
    )


def finish_kernel(rows, groups, in_ref, out_ref, square_ref):
    width = in_ref.shape[1]
    total_square = jnp.zeros((1, 1), F32)
    for group in range(groups):
        total = jnp.zeros((rows, width), F32)
        for block in range(group, in_ref.shape[0] // rows, groups):
            total += in_ref[block * rows : (block + 1) * rows, :].astype(F32)
        out_ref[:, group * width : (group + 1) * width] = total
        total_square += jnp.sum(total * total)
    square_ref[...] = jnp.broadcast_to(total_square, square_ref.shape)


def finish_shard(arrived, rows, groups):
    width = arrived.shape[1]
    shard, square = run_kernel(
        functools.partial(finish_kernel, rows, groups),
        (1,),
        [fixed(arrived.shape)],
        [fixed((rows, width * groups)), fixed((8, 128))],
        [
            jax.ShapeDtypeStruct((rows, width * groups), F32),
            jax.ShapeDtypeStruct((8, 128), F32),
        ],
    )(arrived)
    return shard, square


AXES = ("fsdp", "tp")
PAIR = 2


def swap(value, fsdp_mask, tp_mask, odd_masks=None):
    fsdp_ways, tp_ways = lax.axis_size("fsdp"), lax.axis_size("tp")
    pairs = []
    for row in range(fsdp_ways):
        for col in range(tp_ways):
            masks = (fsdp_mask, tp_mask)
            if odd_masks is not None and col & 1:
                masks = odd_masks
            pairs.append((row * tp_ways + col, (row ^ masks[0]) * tp_ways + (col ^ masks[1])))
    return lax.ppermute(settle(value), AXES, pairs)


def swap_bit(value, axis, bit):
    return swap(value, bit, 0) if axis == "fsdp" else swap(value, 0, bit)


def my_bit(axis, bit):
    return (lax.axis_index(axis) // bit) % 2


def bits_of(ways):
    return [1 << power for power in reversed(range(ways.bit_length() - 1))]


def trade_far(blocks):
    ways = lax.axis_size("fsdp")
    groups = [list(range(side, ways, 2)) for side in range(2)]
    return lax.all_to_all(settle(blocks), "fsdp", 0, 0, axis_index_groups=groups, tiled=True)


def cross(value):
    return swap(value, 1, 0)


def swap_one(value):
    return swap(value, 0, 2, (PAIR, 0))


def swap_two(value):
    return swap(value, PAIR, 0, (0, 2))


def gather_slot(block, other):
    other = settle(other)
    me = lax.axis_index("tp")
    near, far = swap(block, 0, 1), swap(other, 0, 1)
    return arrange([block, other, near, far], [me, me ^ 2, me ^ 1, me ^ 3])


def slot_kernel(x_ref, w_ref, order_ref, *outs):
    rows = outs[0].shape[0]
    place = order_ref[pl.program_id(0)]
    left = x_ref[pl.ds(pl.multiple_of(place * rows, rows), rows), :]
    for number, out_ref in enumerate(outs):

        @pl.when(pl.program_id(0) == number)
        def _(out_ref=out_ref):
            for start in range(0, out_ref.shape[1], TILE):
                here = slice(start, start + TILE)
                out_ref[:, here] = dot_last(left, w_ref[here, :]).astype(BF16)


def slot_product(left, weight):
    me = lax.axis_index("tp")
    rows = left.shape[0] // 4
    cols = weight_shape(weight)[0]
    order = jnp.stack([me ^ 3, me ^ 1, me ^ 2, me]).astype(jnp.int32)
    return run_weights(
        slot_kernel,
        (4,),
        [(fixed(left.shape), left)],
        [weight],
        [(pl.BlockSpec(memory_space=pltpu.SMEM), order)],
        [fixed((rows, cols))] * 4,
        [jax.ShapeDtypeStruct((rows, cols), BF16)] * 4,
    )


def sum_everywhere(value):
    for bit in bits_of(lax.axis_size("tp"))[::-1]:
        value = value + swap(value, 0, bit)
    for bit in bits_of(lax.axis_size("fsdp")):
        value = value + swap(value, bit, 0)
    return value


def on_device(
    tokens,
    out_grad,
    lengths,
    w_query,
    w_key,
    w_value,
    w_out,
    w_gate,
    w_up,
    w_down,
    norm_attn,
    norm_mlp,
    moment_query,
    moment_key,
    moment_value,
    moment_out,
    moment_gate,
    moment_up,
    moment_down,
    moment_norm_attn,
    moment_norm_mlp,
    square_query,
    square_key,
    square_value,
    square_out,
    square_gate,
    square_up,
    square_down,
    square_norm_attn,
    square_norm_mlp,
):
    rows_dev = tokens.shape[0]
    tp_ways = lax.axis_size("tp")
    slot_rows = rows_dev * tp_ways
    heads, heads_kv = w_query.shape[1] // HD, w_key.shape[1] // HD
    shard_rows = w_query.shape[0]
    length = lengths[0]
    row_pos = lax.axis_index("tp") * rows_dev + jnp.arange(rows_dev)
    gain_attn, gain_mlp = norm_attn[None], norm_mlp[None]
    far_rows = shard_rows * (lax.axis_size("fsdp") // 2)

    normed_attn = enter_norm(tokens, gain_attn)
    slot_other = swap(normed_attn, 0, 2)
    qkv_blocks = spread([pin(w_query, normed_attn), w_key, w_value], 1)
    qkv_rows = trade_far(qkv_blocks)
    out_blocks = spread([pin(w_out, qkv_blocks)], 1)
    gate_blocks = spread([pin(w_gate, out_blocks)], 2)
    cosine_table, sine_table = rotary_tables(slot_rows, HD)
    full_qkv = (qkv_rows, cross(qkv_rows))
    cotangent = jnp.where(row_pos[:, None] < length, out_grad, jnp.zeros_like(out_grad))
    grad_pair = swap(cotangent, PAIR, 0)
    attn_input = gather_slot(normed_attn, pin(slot_other, grad_pair))
    out_rows = trade_far(pin(out_blocks, qkv_rows, slot_other))
    full_out = (out_rows, cross(out_rows))
    grad_other, grad_both = swap(cotangent, 0, 2), swap(grad_pair, 0, 2)
    gate_rows = trade_far(pin(gate_blocks, out_rows))

    qkv_rot = project_qkv(pin(attn_input, out_rows), full_qkv, cosine_table, sine_table, heads + heads_kv)
    odd = my_bit("tp", 1)
    grad_mine = arrange(
        [pin(cotangent, qkv_rot), grad_other, grad_pair, grad_both], [0, 1 + odd, 2 - odd, 3]
    )
    grad_near = swap(grad_mine, 0, 1)
    up_blocks = spread([pin(w_up, qkv_rot)], 2)
    attn_bf = attend(pin(qkv_rot, up_blocks), lengths, heads, heads_kv)
    attn_parts = slot_product(pin(attn_bf, grad_mine), full_out)
    attn_got = [swap(part, 0, 1) for part in attn_parts[:2]]
    attn_sent = add_low(rows_dev, (attn_parts[2], 0), (attn_got[0], 0))
    attn_last = swap(attn_sent, 0, 2)
    gate_rows = settle(pin(gate_rows, attn_sent))
    gate_crossed = cross(gate_rows)
    full_gate = (gate_rows, gate_crossed)
    up_rows = trade_far(pin(up_blocks, gate_rows))
    down_blocks = spread([pin(w_down, attn_sent)], 2)
    middle, normed_mlp = middle_norm(
        rows_dev,
        [
            (tokens, 0),
            (attn_parts[3], 0),
            (attn_got[1], 0),
            (pin(attn_last, down_blocks, grad_near), 0),
        ],
        gain_mlp,
    )
    first = swap_one(normed_mlp)
    second = swap_two(normed_mlp)
    up_rows = settle(pin(up_rows, first, gate_crossed))
    up_crossed = cross(up_rows)
    full_up = (up_rows, up_crossed)
    both = swap_two(first)
    mlp_mine = arrange([normed_mlp, first, second, pin(both, up_crossed)], range(4))
    near_blocks = [swap(one, 0, 1) for one in (normed_mlp, first, second)]
    near_blocks.append(swap(pin(both, up_crossed), 0, 1))
    mlp_near = arrange(near_blocks, range(4))
    down_rows = trade_far(pin(down_blocks, up_rows, both, second))
    hid_mine, upp_mine, gatep_mine = mlp_forward(mlp_mine, full_gate, full_up)
    down_rows = settle(pin(down_rows, hid_mine))
    full_down = (down_rows, cross(down_rows))
    hid_near, upp_near, gatep_near = mlp_forward(pin(mlp_near, down_rows), full_gate, full_up)

    down_sent, down_own = weight_grad([grad_mine, grad_near], [hid_mine, hid_near])
    down_got = cross(down_sent)
    dgate_near, dup_near = mlp_backward(pin(grad_near, down_own), full_down, upp_near, gatep_near)
    dgate_mine, dup_mine = mlp_backward(
        pin(grad_mine, dgate_near), full_down, upp_mine, gatep_mine
    )
    gate_sent, gate_own = weight_grad([mlp_mine, mlp_near], [dgate_mine, dgate_near])
    gate_got = cross(gate_sent)
    up_sent, up_own = weight_grad([pin(mlp_mine, gate_own), mlp_near], [dup_mine, dup_near])
    up_got = cross(up_sent)
    down_far = trade_far(add_low(far_rows, (pin(down_got, gate_own), 0), (down_own, 0)))
    back_near = back_product(pin(dgate_near, up_own), dup_near, full_gate, full_up, parts=4)
    back_got = [swap(part, 0, 1) for part in back_near]
    back_mine = back_product(pin(dgate_mine, back_near[0], gate_got), dup_mine, full_gate, full_up, parts=4)
    sent = [add_low(rows_dev, (back_mine[one], 0), (back_got[one], 0)) for one in (2, 3)]
    back_two = [swap_two(one) for one in sent]
    (out_near,) = back_product(pin(hid_near, *sent), full_down)
    (out_mine,) = back_product(pin(hid_mine, out_near), full_down)
    sent = add_low(
        rows_dev, (back_mine[1], 0), (back_got[1], 0), (pin(back_two[1], out_mine, down_far), 0)
    )
    back_one = swap_one(sent)
    out_got = swap(pin(out_near, sent), 0, 1)
    gate_far = trade_far(add_low(far_rows, (pin(gate_got, sent), 0), (gate_own, 0)))
    middle_grad, low_grad, gain_mlp_part = leave_norm(
        rows_dev,
        [(back_mine[0], 0), (back_got[0], 0), (back_two[0], 0), (pin(back_one, up_got), 0)],
        middle,
        cotangent,
        gain_mlp,
        [F32, BF16],
    )
    slot_other = swap(low_grad, 0, 2)
    attn_grad_in = gather_slot(low_grad, slot_other)
    proj_sent, proj_own = weight_grad([attn_grad_in], [attn_bf])
    proj_got = cross(proj_sent)
    query_grad, key_grad, value_grad = attend_back(
        pin(attn_grad_in, proj_own, gate_far),
        full_out, qkv_rot, lengths, cosine_table, sine_table, heads, heads_kv,
    )
    up_far = trade_far(add_low(far_rows, (pin(up_got, attn_grad_in, gate_far), 0), (up_own, 0)))
    shard_down, square_down_part = finish_shard(pin(down_far, query_grad), shard_rows, 2)
    sent = add_low(
        2 * rows_dev, (out_mine, 2 * rows_dev), (pin(out_got, query_grad), 2 * rows_dev)
    )
    out_two = swap_two(sent)
    qkv_grad = jnp.concatenate([query_grad, key_grad, value_grad], axis=1)
    qkv_sent, qkv_own = weight_grad([attn_input], [qkv_grad])
    qkv_got = cross(qkv_sent)
    input_parts = slot_product(pin(qkv_grad, qkv_own, proj_got), full_qkv)
    input_got = [swap(part, 0, 1) for part in input_parts[:2]]
    proj_low = add_low(far_rows, (pin(proj_got, up_far, input_parts[3]), 0), (proj_own, 0))
    proj_far = trade_far(proj_low)
    sent = add_low(
        rows_dev, (out_mine, rows_dev), (out_got, rows_dev), (pin(out_two, proj_low), rows_dev)
    )
    out_one = swap_one(sent)
    input_sent = add_low(
        rows_dev, (input_parts[2], 0), (pin(input_got[0], sent, qkv_got), 0)
    )
    input_last = swap(input_sent, 0, 2)
    shard_gate, square_gate_part = finish_shard(pin(gate_far, input_sent), shard_rows, 2)
    shard_up, square_up_part = finish_shard(pin(up_far, input_sent), shard_rows, 2)
    qkv_far = trade_far(add_low(far_rows, (pin(qkv_got, proj_far), 0), (qkv_own, 0)))
    input_grad, gain_attn_part = leave_norm(
        rows_dev,
        [(input_parts[3], 0), (input_got[1], 0), (pin(input_last, shard_gate, shard_up), 0)],
        tokens,
        middle_grad,
        gain_attn,
        [F32],
    )
    block_out = add_low(
        rows_dev,
        (middle, 0),
        (out_mine, 0),
        (out_got, 0),
        (out_two, 0),
        (pin(out_one, input_grad), 0),
    )
    gains = jnp.concatenate([gain_attn_part[0], gain_mlp_part[0]]).reshape(-1, 128)
    gains = sum_everywhere(gains).reshape(-1)
    shard_out, square_out_part = finish_shard(proj_far, shard_rows, 1)
    shard_qkv, square_qkv_part = finish_shard(qkv_far, shard_rows, 1)
    width_query, width_key = w_query.shape[1], w_key.shape[1]
    shard_grads = (
        shard_qkv[:, :width_query],
        shard_qkv[:, width_query : width_query + width_key],
        shard_qkv[:, width_query + width_key :],
        shard_out,
        shard_gate,
        shard_up,
        shard_down,
    )
    square_part = (
        square_down_part + square_gate_part + square_up_part + square_qkv_part + square_out_part
    )
    square_total = sum_everywhere(square_part)[0, 0]
    gain_attn_grad = gains[: norm_attn.shape[0]]
    gain_mlp_grad = gains[norm_attn.shape[0] :]
    clip_norm = jnp.sqrt(
        square_total
        + jnp.sum(gain_attn_grad * gain_attn_grad)
        + jnp.sum(gain_mlp_grad * gain_mlp_grad)
    )
    factor = jnp.minimum(1.0, MAX_NORM / (clip_norm + 1e-06))
    every_grad = tuple(shard_grads) + (gain_attn_grad, gain_mlp_grad)
    params = (w_query, w_key, w_value, w_out, w_gate, w_up, w_down, norm_attn, norm_mlp)
    moments = (
        moment_query,
        moment_key,
        moment_value,
        moment_out,
        moment_gate,
        moment_up,
        moment_down,
        moment_norm_attn,
        moment_norm_mlp,
    )
    squares = (
        square_query,
        square_key,
        square_value,
        square_out,
        square_gate,
        square_up,
        square_down,
        square_norm_attn,
        square_norm_mlp,
    )
    results = [
        adam_step(params[number], every_grad[number], moments[number], squares[number], factor)
        for number in range(9)
    ]
    return (
        block_out,
        input_grad,
        every_grad[0],
        every_grad[1],
        every_grad[2],
        every_grad[3],
        every_grad[4],
        every_grad[5],
        every_grad[6],
        every_grad[7],
        every_grad[8],
        results[0][0],
        results[1][0],
        results[2][0],
        results[3][0],
        results[4][0],
        results[5][0],
        results[6][0],
        results[7][0],
        results[8][0],
        results[0][1],
        results[1][1],
        results[2][1],
        results[3][1],
        results[4][1],
        results[5][1],
        results[6][1],
        results[7][1],
        results[8][1],
        results[0][2],
        results[1][2],
        results[2][2],
        results[3][2],
        results[4][2],
        results[5][2],
        results[6][2],
        results[7][2],
        results[8][2],
        clip_norm,
    )


def solution(mesh):
    return jax.shard_map(
        on_device,
        mesh=mesh,
        in_specs=(
            P(("fsdp", "tp"), None),
            P(("fsdp", "tp"), None),
            P("fsdp"),
            P("fsdp", "tp"),
            P("fsdp", "tp"),
            P("fsdp", "tp"),
            P("fsdp", "tp"),
            P("fsdp", "tp"),
            P("fsdp", "tp"),
            P("fsdp", "tp"),
            P(),
            P(),
            P("fsdp", "tp"),
            P("fsdp", "tp"),
            P("fsdp", "tp"),
            P("fsdp", "tp"),
            P("fsdp", "tp"),
            P("fsdp", "tp"),
            P("fsdp", "tp"),
            P(),
            P(),
            P("fsdp", "tp"),
            P("fsdp", "tp"),
            P("fsdp", "tp"),
            P("fsdp", "tp"),
            P("fsdp", "tp"),
            P("fsdp", "tp"),
            P("fsdp", "tp"),
            P(),
            P(),
        ),
        out_specs=(
            P(("fsdp", "tp"), None),
            P(("fsdp", "tp"), None),
            P("fsdp", "tp"),
            P("fsdp", "tp"),
            P("fsdp", "tp"),
            P("fsdp", "tp"),
            P("fsdp", "tp"),
            P("fsdp", "tp"),
            P("fsdp", "tp"),
            P(),
            P(),
            P("fsdp", "tp"),
            P("fsdp", "tp"),
            P("fsdp", "tp"),
            P("fsdp", "tp"),
            P("fsdp", "tp"),
            P("fsdp", "tp"),
            P("fsdp", "tp"),
            P(),
            P(),
            P("fsdp", "tp"),
            P("fsdp", "tp"),
            P("fsdp", "tp"),
            P("fsdp", "tp"),
            P("fsdp", "tp"),
            P("fsdp", "tp"),
            P("fsdp", "tp"),
            P(),
            P(),
            P("fsdp", "tp"),
            P("fsdp", "tp"),
            P("fsdp", "tp"),
            P("fsdp", "tp"),
            P("fsdp", "tp"),
            P("fsdp", "tp"),
            P("fsdp", "tp"),
            P(),
            P(),
            P(),
        ),
        check_vma=False,
    )
```

```python
import functools

import jax
import jax.numpy as jnp
from jax import lax
from jax.experimental import pallas as pl
from jax.experimental.pallas import tpu as pltpu
from jax.sharding import PartitionSpec as P

HD = 256
STEP = 10


EPS_NORM = 1e-05
THETA = 1000042.0
LEARN_RATE = 0.02
BETA_ONE = 0.9
BETA_TWO = 0.95
ADAM_EPS = 1e-08
WEIGHT_DECAY = 0.1
MAX_NORM = 1.0
MASKED = -1000000000.0


def rotary_tables(count, head_dim):
    positions = jnp.arange(count).astype(jnp.float32)
    inverse = THETA ** (-2.0 * jnp.arange(head_dim // 2).astype(jnp.float32) / head_dim)
    angles = positions[:, None] * inverse[None, :]
    return (jnp.cos(angles), jnp.sin(angles))


def dot_rows(left, right):
    return lax.dot_general(
        left, right, (((0,), (0,)), ((), ())), preferred_element_type=jnp.float32
    )


def dot_last(left, right):
    return lax.dot_general(
        left, right, (((1,), (1,)), ((), ())), preferred_element_type=jnp.float32
    )


def adam_step(master, gradient, moment, square, factor):
    clipped = gradient * factor
    new_moment = BETA_ONE * moment + (1.0 - BETA_ONE) * clipped
    new_square = BETA_TWO * square + (1.0 - BETA_TWO) * clipped * clipped
    moment_hat = new_moment / (1.0 - BETA_ONE**STEP)
    square_hat = new_square / (1.0 - BETA_TWO**STEP)
    update = -LEARN_RATE * (moment_hat / (jnp.sqrt(square_hat) + ADAM_EPS) + WEIGHT_DECAY * master)
    return (new_moment, new_square, update)


F32, BF16 = jnp.float32, jnp.bfloat16
TILE = 256
VMEM_BYTES = 48 * 1024 * 1024
SMALL_COST = pl.CostEstimate(flops=1, bytes_accessed=1, transcendentals=0)


class Pinned:
    def __init__(self, value, before):
        self.value, self.before = value, before
        self.shape, self.dtype = value.shape, value.dtype


def pin(value, *before):
    if isinstance(value, Pinned):
        return Pinned(value.value, (*value.before, *before))
    return Pinned(value, before)


def unpin(operands):
    arrays, before = [], []
    for one in operands:
        if isinstance(one, Pinned):
            before += [other for other in one.before if all(other is not had for had in before)]
            one = one.value
        arrays.append(one)
    return arrays, before


def call_kernel(kernel, grid_spec, out_shape, operands, scalars=0, aliases=()):
    arrays, before = unpin(operands)
    count, spare = len(arrays), len(before)

    def body(*refs):
        kernel(*refs[:count], *refs[count + spare :])

    spec = pltpu.PrefetchScalarGridSpec(
        num_scalar_prefetch=scalars,
        grid=grid_spec["grid"],
        in_specs=list(grid_spec["in_specs"]) + [pl.BlockSpec(memory_space=pl.ANY)] * spare,
        out_specs=grid_spec["out_specs"],
        scratch_shapes=grid_spec.get("scratch", ()),
    )
    return pl.pallas_call(
        body,
        grid_spec=spec,
        out_shape=out_shape,
        input_output_aliases=dict(aliases),
        compiler_params=pltpu.CompilerParams(
            dimension_semantics=("arbitrary",) * len(grid_spec["grid"]),
            vmem_limit_bytes=VMEM_BYTES,
        ),
        cost_estimate=SMALL_COST,
    )(*arrays, *before)


def run_kernel(kernel, grid, in_specs, out_specs, out_shape, scratch=()):
    def call(*operands):
        spec = {"grid": grid, "in_specs": in_specs, "out_specs": out_specs, "scratch": scratch}
        return call_kernel(kernel, spec, out_shape, operands)

    return call


def hold_kernel(value_ref, out_ref):
    del value_ref, out_ref


def settle(value):
    if not isinstance(value, Pinned):
        return value
    anywhere = pl.BlockSpec(memory_space=pl.ANY)
    return call_kernel(
        hold_kernel,
        {"grid": (1,), "in_specs": [anywhere], "out_specs": anywhere},
        jax.ShapeDtypeStruct(value.shape, value.dtype),
        [value],
        aliases=((0, 0),),
    )


def weight_shape(weight):
    return (weight[0].shape[0] * 2, weight[0].shape[1])


def with_weights(weights, places, body, first_step, *refs):
    side_ref, refs = refs[0], list(refs[1:])
    scratch = refs[len(refs) - 2 * len(weights) :]
    refs = refs[: len(refs) - 2 * len(weights)]
    count = sum(len(weight) for weight in weights)
    held = refs[places : places + count]
    rest = refs[:places] + refs[places + count :]
    ways = lax.axis_size("fsdp")

    @pl.when(first_step())
    def _():
        copies = []
        for number, weight in enumerate(weights):
            rows = weight_shape(weight)[0] // ways
            block = 0
            for part in weight:
                ref = held.pop(0)
                for place in range(part.shape[0] // rows):
                    other, index = divmod(block, ways // 2)
                    row = pl.multiple_of((2 * index + (side_ref[0] ^ other)) * rows, rows)
                    copies.append(
                        pltpu.make_async_copy(
                            ref.at[pl.ds(place * rows, rows), :],
                            scratch[2 * number].at[pl.ds(row, rows), :],
                            scratch[2 * number + 1].at[block],
                        )
                    )
                    block += 1
        for copy in copies:
            copy.start()
        for copy in copies:
            copy.wait()

    body(*rest[:places], *scratch[0::2], *rest[places:])


def run_weights(body, grid, before, weights, after, out_specs, out_shape, scratch=()):
    side = my_bit("fsdp", 1).astype(jnp.int32).reshape((1,))
    spare = []
    for weight in weights:
        spare += [
            pltpu.VMEM(weight_shape(weight), BF16),
            pltpu.SemaphoreType.DMA((lax.axis_size("fsdp"),)),
        ]

    def first_step():
        first = pl.program_id(0) == 0
        for axis in range(1, len(grid)):
            first = first & (pl.program_id(axis) == 0)
        return first

    return run_kernel(
        functools.partial(with_weights, weights, len(before), body, first_step),
        grid,
        [pl.BlockSpec(memory_space=pltpu.SMEM)]
        + [spec for spec, _ in before]
        + [pl.BlockSpec(memory_space=pl.ANY)] * sum(len(weight) for weight in weights)
        + [spec for spec, _ in after],
        out_specs,
        out_shape,
        list(scratch) + spare,
    )(
        side,
        *[one for _, one in before],
        *[part for weight in weights for part in weight],
        *[one for _, one in after],
    )


def fixed(shape):
    return pl.BlockSpec(shape, lambda *_: (0,) * len(shape))


def by_rows(cols):
    return pl.BlockSpec((TILE, cols), lambda step: (step, 0))


def dot_plain(left, right):
    return jnp.dot(left, right, preferred_element_type=F32)


def qkv_kernel(rotated, x_ref, w_ref, cos_ref, sin_ref, out_ref):
    half = HD // 2
    cosine, sine = cos_ref[...], sin_ref[...]
    for head in range(w_ref.shape[1] // HD):
        here = slice(head * HD, (head + 1) * HD)
        lin = dot_plain(x_ref[...], w_ref[:, here])
        if head < rotated:
            first, second = lin[:, :half], lin[:, half:]
            out_ref[:, head * HD : head * HD + half] = (first * cosine - second * sine).astype(BF16)
            out_ref[:, head * HD + half : (head + 1) * HD] = (
                second * cosine + first * sine
            ).astype(BF16)
        else:
            out_ref[:, here] = lin.astype(BF16)


def project_qkv(attn_input, full_qkv, cosine_table, sine_table, rotated):
    rows, depth = attn_input.shape
    cols = weight_shape(full_qkv)[1]
    return run_weights(
        functools.partial(qkv_kernel, rotated),
        (rows // TILE,),
        [(by_rows(depth), attn_input)],
        [full_qkv],
        [(by_rows(HD // 2), cosine_table), (by_rows(HD // 2), sine_table)],
        by_rows(cols),
        jax.ShapeDtypeStruct((rows, cols), BF16),
    )


def soft_rows(query, keys, first_row, length):
    scores = dot_last(query, keys) * (HD**-0.5)
    rows = first_row + lax.broadcasted_iota(jnp.int32, scores.shape, 0)
    cols = lax.broadcasted_iota(jnp.int32, scores.shape, 1)
    scores = jnp.where((cols <= rows) & (cols < length), scores, MASKED)
    exponent = jnp.exp(scores - jnp.max(scores, axis=-1, keepdims=True))
    return exponent / jnp.sum(exponent, axis=-1, keepdims=True)


def attend_kernel(blocks, length_ref, q_ref, k_ref, v_ref, out_ref):
    for block in range(blocks):

        @pl.when(pl.program_id(1) == block)
        def _():
            width = (block + 1) * TILE
            probs = soft_rows(q_ref[...], k_ref[:width, :], block * TILE, length_ref[0])
            out_ref[...] = dot_plain(probs.astype(BF16), v_ref[:width, :]).astype(BF16)


def attend(qkv_rot, lengths, heads, heads_kv):
    rows = qkv_rot.shape[0]
    group = heads // heads_kv
    blocks = rows // TILE
    return run_kernel(
        functools.partial(attend_kernel, blocks),
        (heads, blocks),
        [
            pl.BlockSpec(memory_space=pltpu.SMEM),
            pl.BlockSpec((TILE, HD), lambda head, step: (step, head)),
            pl.BlockSpec((rows, HD), lambda head, step: (0, heads + head // group)),
            pl.BlockSpec((rows, HD), lambda head, step: (0, heads + heads_kv + head // group)),
        ],
        pl.BlockSpec((TILE, HD), lambda head, step: (step, head)),
        jax.ShapeDtypeStruct((rows, heads * HD), BF16),
    )(lengths, qkv_rot, qkv_rot, qkv_rot)


def attend_back_kernel(
    blocks, group, x_ref, w_ref, length_ref, q_ref, k_ref, v_ref, cos_ref, sin_ref,
    cos_all, sin_all, dq_ref, dk_ref, dv_ref, dk_sum, dv_sum,
):
    half = HD // 2
    step, member = pl.program_id(1), pl.program_id(2)

    @pl.when((step == 0) & (member == 0))
    def _():
        dk_sum[...] = jnp.zeros_like(dk_sum)
        dv_sum[...] = jnp.zeros_like(dv_sum)

    def unrotate(value, cosine, sine):
        first, second = value[:, :half], value[:, half:]
        return jnp.concatenate(
            [first * cosine + second * sine, second * cosine - first * sine], axis=1
        ).astype(BF16)

    for block in range(blocks):

        @pl.when(step == block)
        def _():
            width = (block + 1) * TILE
            query, keys, values = q_ref[...], k_ref[:width, :], v_ref[:width, :]
            here = pl.multiple_of((pl.program_id(0) * group + member) * HD, HD)
            grad = dot_plain(x_ref[...], w_ref[:, pl.ds(here, HD)]).astype(BF16)
            probs = soft_rows(query, keys, block * TILE, length_ref[0])
            prob_grad = dot_last(grad, values)
            delta = jnp.sum(probs * prob_grad, axis=-1, keepdims=True)
            score_grad = (probs * (prob_grad - delta) * (HD**-0.5)).astype(BF16)
            dq_ref[...] = unrotate(dot_plain(score_grad, keys), cos_ref[...], sin_ref[...])
            dk_sum[:width, :] += dot_rows(score_grad, query)
            dv_sum[:width, :] += dot_rows(probs.astype(BF16), grad)

    @pl.when((step == blocks - 1) & (member == group - 1))
    def _():
        dk_ref[...] = unrotate(dk_sum[...], cos_all[...], sin_all[...])
        dv_ref[...] = dv_sum[...].astype(BF16)


def attend_back(attn_grad_in, full_out, qkv_rot, lengths, cosine_table, sine_table, heads, heads_kv):
    rows, depth = attn_grad_in.shape
    group = heads // heads_kv
    blocks = rows // TILE
    half = HD // 2
    return run_weights(
        functools.partial(attend_back_kernel, blocks, group),
        (heads_kv, blocks, group),
        [(pl.BlockSpec((TILE, depth), lambda kv, step, one: (step, 0)), attn_grad_in)],
        [full_out],
        [
            (pl.BlockSpec(memory_space=pltpu.SMEM), lengths),
            (pl.BlockSpec((TILE, HD), lambda kv, step, one: (step, kv * group + one)), qkv_rot),
            (pl.BlockSpec((rows, HD), lambda kv, step, one: (0, heads + kv)), qkv_rot),
            (pl.BlockSpec((rows, HD), lambda kv, step, one: (0, heads + heads_kv + kv)), qkv_rot),
            (pl.BlockSpec((TILE, half), lambda kv, step, one: (step, 0)), cosine_table),
            (pl.BlockSpec((TILE, half), lambda kv, step, one: (step, 0)), sine_table),
            (fixed((rows, half)), cosine_table),
            (fixed((rows, half)), sine_table),
        ],
        [
            pl.BlockSpec((TILE, HD), lambda kv, step, one: (step, kv * group + one)),
            pl.BlockSpec((rows, HD), lambda kv, step, one: (0, kv)),
            pl.BlockSpec((rows, HD), lambda kv, step, one: (0, kv)),
        ],
        [
            jax.ShapeDtypeStruct((rows, heads * HD), BF16),
            jax.ShapeDtypeStruct((rows, heads_kv * HD), BF16),
            jax.ShapeDtypeStruct((rows, heads_kv * HD), BF16),
        ],
        [pltpu.VMEM((rows, HD), F32), pltpu.VMEM((rows, HD), F32)],
    )


def mlp_kernel(x_ref, gate_ref, up_ref, hidden_ref, up_part_ref, gate_part_ref):
    for start in range(0, gate_ref.shape[1], TILE):
        here = slice(start, start + TILE)
        gate = dot_plain(x_ref[...], gate_ref[:, here])
        up = dot_plain(x_ref[...], up_ref[:, here])
        sig = jax.nn.sigmoid(gate)
        act = gate * sig
        hidden_ref[:, here] = (act * up).astype(BF16)
        gate_part_ref[:, here] = (up * sig * (1.0 + gate * (1.0 - sig))).astype(BF16)
        up_part_ref[:, here] = act.astype(BF16)


def mlp_forward(block, full_gate, full_up):
    rows, depth = block.shape
    cols = weight_shape(full_gate)[1]
    return run_weights(
        mlp_kernel,
        (rows // TILE,),
        [(by_rows(depth), block)],
        [full_gate, full_up],
        [],
        [by_rows(cols)] * 3,
        [jax.ShapeDtypeStruct((rows, cols), BF16)] * 3,
    )


def mlp_grad_kernel(x_ref, down_ref, up_part_ref, gate_part_ref, gate_ref, up_ref):
    for start in range(0, down_ref.shape[1], TILE):
        here = slice(start, start + TILE)
        hidden_grad = dot_plain(x_ref[...], down_ref[:, here])
        gate_ref[:, here] = (hidden_grad * gate_part_ref[:, here].astype(F32)).astype(BF16)
        up_ref[:, here] = (hidden_grad * up_part_ref[:, here].astype(F32)).astype(BF16)


def mlp_backward(block, full_down, up_part, gate_part):
    rows, depth = block.shape
    cols = weight_shape(full_down)[1]
    return run_weights(
        mlp_grad_kernel,
        (rows // TILE,),
        [(by_rows(depth), block)],
        [full_down],
        [(by_rows(cols), up_part), (by_rows(cols), gate_part)],
        [by_rows(cols)] * 2,
        [jax.ShapeDtypeStruct((rows, cols), BF16)] * 2,
    )


def back_kernel(count, tiles, *refs):
    lefts, rights, outs = refs[:count], refs[count : 2 * count], refs[2 * count :]

    def write(out_ref):
        for start in range(0, out_ref.shape[1], TILE):
            here = slice(start, start + TILE)
            total = dot_last(lefts[0][...], rights[0][here, :])
            for number in range(1, count):
                total += dot_last(lefts[number][...], rights[number][here, :])
            out_ref[:, here] = total.astype(BF16)

    for number in range(len(outs)):
        first, last = number * tiles, (number + 1) * tiles

        @pl.when((pl.program_id(0) >= first) & (pl.program_id(0) < last))
        def _(number=number):
            write(outs[number])


def back_product(*operands, parts=1):
    count = len(operands) // 2
    lefts, rights = operands[:count], operands[count:]
    rows = lefts[0].shape[0]
    cols = weight_shape(rights[0])[0]
    tiles = rows // TILE // parts
    return run_weights(
        functools.partial(back_kernel, count, tiles),
        (rows // TILE,),
        [(by_rows(left.shape[1]), left) for left in lefts],
        list(rights),
        [],
        [
            pl.BlockSpec(
                (TILE, cols), lambda step, part=part: (jnp.clip(step - part * tiles, 0, tiles - 1), 0)
            )
            for part in range(parts)
        ],
        [jax.ShapeDtypeStruct((rows // parts, cols), BF16)] * parts,
    )


def arrange_kernel(parts, place_ref, *refs):
    for number in range(parts):

        @pl.when(pl.program_id(0) == number)
        def _():
            refs[parts][...] = refs[number][...]


def arrange(parts, places):
    rows, width = parts[0].shape
    count = len(parts)
    place = {
        "grid": (count,),
        "in_specs": [pl.BlockSpec((rows, width), lambda step, place: (0, 0))] * count,
        "out_specs": pl.BlockSpec((rows, width), lambda step, place: (place[step], 0)),
    }
    return call_kernel(
        functools.partial(arrange_kernel, count),
        place,
        jax.ShapeDtypeStruct((rows * count, width), parts[0].dtype),
        [jnp.stack([jnp.asarray(one, jnp.int32) for one in places]), *parts],
        scalars=1,
    )


def rowwise_kernel(fn, operands, outs, *refs):
    results = fn(*[ref[...] for ref in refs[:operands]])
    targets = refs[operands:]
    for number in range(outs):
        targets[number][...] = results[number].astype(targets[number].dtype)
    for number in range(outs, len(targets)):
        partial = jnp.broadcast_to(
            jnp.sum(results[number], axis=0, keepdims=True), targets[number].shape
        )

        @pl.when(pl.program_id(0) == 0)
        def _(number=number, partial=partial):
            targets[number][...] = partial

        @pl.when(pl.program_id(0) > 0)
        def _(number=number, partial=partial):
            targets[number][...] += partial


def rowwise(fn, rows, operands, outs, sums=0):
    tile = rows // 4
    specs = []
    for array, first in operands:
        cols = array.shape[1]
        if first is None:
            specs.append(fixed(array.shape))
        else:
            specs.append(pl.BlockSpec((tile, cols), lambda step, at=first // tile: (step + at, 0)))
    cols = operands[0][0].shape[1]
    return run_kernel(
        functools.partial(rowwise_kernel, fn, len(operands), len(outs)),
        (4,),
        specs,
        [pl.BlockSpec((tile, cols), lambda step: (step, 0))] * len(outs) + [fixed((8, cols))] * sums,
        [jax.ShapeDtypeStruct((rows, cols), one) for one in outs]
        + [jax.ShapeDtypeStruct((8, cols), F32)] * sums,
    )(*[array for array, _ in operands])


def sum_tiles(*tiles):
    total = tiles[0].astype(F32)
    for tile in tiles[1:]:
        total = total + tile.astype(F32)
    return total


def add_low(rows, *operands):
    return rowwise(lambda *tiles: (sum_tiles(*tiles),), rows, operands, [BF16])[0]


def row_scale_of(values):
    return lax.rsqrt(jnp.mean(values * values, axis=-1, keepdims=True) + EPS_NORM)


def enter_norm(tokens, gain):
    def body(values, gain):
        values = values.astype(F32)
        return (values * row_scale_of(values) * gain,)

    return rowwise(body, tokens.shape[0], [(tokens, 0), (gain, None)], [BF16])[0]


def middle_norm(rows, operands, gain):
    def body(*tiles):
        values = sum_tiles(*tiles[:-1])
        return values, values * row_scale_of(values) * tiles[-1]

    return rowwise(body, rows, [*operands, (gain, None)], [F32, BF16])


def leave_norm(rows, operands, values, passed, gain, outs):
    def body(*tiles):
        incoming = sum_tiles(*tiles[:-3])
        values, passed, gain = tiles[-3].astype(F32), tiles[-2].astype(F32), tiles[-1]
        scale = row_scale_of(values)
        weighted = incoming * gain
        mean = jnp.mean(weighted * values, axis=-1, keepdims=True)
        result = passed + scale * weighted - values * scale**3 * mean
        return *[result for _ in outs], incoming * values * scale

    return rowwise(body, rows, [*operands, (values, 0), (passed, 0), (gain, None)], outs, 1)


def spread_kernel(count, groups, *refs):
    weights, out_ref = refs[:count], refs[-1]
    if groups == 1:
        start = 0
        for weight in weights:
            width = weight.shape[1]
            out_ref[:, start : start + width] = weight[...].astype(BF16)
            start += width
    else:
        width = out_ref.shape[1]
        for group in range(groups):

            @pl.when(lax.rem(pl.program_id(0), groups) == group)
            def _():
                here = slice(group * width, (group + 1) * width)
                out_ref[...] = weights[0][:, here].astype(BF16)


def spread(weights, groups):
    ways = lax.axis_size("fsdp") // 2
    rows = weights[0].shape[0]
    width = sum(weight.shape[1] for weight in weights) // groups
    return run_kernel(
        functools.partial(spread_kernel, len(weights), groups),
        (ways,),
        [fixed(weight.shape) for weight in weights],
        by_rows(width) if rows == TILE else pl.BlockSpec((rows, width), lambda step: (step, 0)),
        jax.ShapeDtypeStruct((ways * rows, width), BF16),
    )(*weights)


def weight_kernel(count, half, order_ref, *refs):
    lefts, rights = refs[:count], refs[count : 2 * count]
    sent_ref, kept_ref = refs[2 * count :]

    def write(out_ref):
        for start in range(0, out_ref.shape[1], TILE):
            here = slice(start, start + TILE)
            total = dot_rows(lefts[0][...], rights[0][:, here])
            for number in range(1, count):
                total += dot_rows(lefts[number][...], rights[number][:, here])
            out_ref[:, here] = total.astype(BF16)

    @pl.when(pl.program_id(0) < half)
    def _():
        write(sent_ref)

    @pl.when(pl.program_id(0) >= half)
    def _():
        write(kept_ref)


def weight_grad(lefts, rights):
    count = len(lefts)
    rows, depth = lefts[0].shape
    cols = rights[0].shape[1]
    ways = lax.axis_size("fsdp")
    block, half = depth // ways, ways // 2
    side = my_bit("fsdp", 1).astype(jnp.int32)
    pairs = 2 * jnp.arange(half, dtype=jnp.int32)
    order = jnp.concatenate([pairs + 1 - side, pairs + side])
    if block % 128:
        lefts = [settle(left) for left in lefts]
        rights = [settle(right) for right in rights]
        total = sum(dot_rows(left, right) for left, right in zip(lefts, rights))
        blocks = total.astype(BF16).reshape(ways, block, cols)[order].reshape(-1, cols)
        return blocks[: block * half], blocks[block * half :]
    place = {
        "grid": (ways,),
        "in_specs": [pl.BlockSpec((rows, block), lambda step, order: (0, order[step]))] * count
        + [pl.BlockSpec((rows, cols), lambda step, order: (0, 0))] * count,
        "out_specs": [
            pl.BlockSpec((block, cols), lambda step, order: (jnp.minimum(step, half - 1), 0)),
            pl.BlockSpec((block, cols), lambda step, order: (jnp.maximum(step - half, 0), 0)),
        ],
    }
    return call_kernel(
        functools.partial(weight_kernel, count, half),
        place,
        [jax.ShapeDtypeStruct((half * block, cols), BF16)] * 2,
        [order, *lefts, *rights],
        scalars=1,
    )


def finish_kernel(rows, groups, in_ref, out_ref, square_ref):
    width = in_ref.shape[1]
    total_square = jnp.zeros((1, 1), F32)
    for group in range(groups):
        total = jnp.zeros((rows, width), F32)
        for block in range(group, in_ref.shape[0] // rows, groups):
            total += in_ref[block * rows : (block + 1) * rows, :].astype(F32)
        out_ref[:, group * width : (group + 1) * width] = total
        total_square += jnp.sum(total * total)
    square_ref[...] = jnp.broadcast_to(total_square, square_ref.shape)


def finish_shard(arrived, rows, groups):
    width = arrived.shape[1]
    shard, square = run_kernel(
        functools.partial(finish_kernel, rows, groups),
        (1,),
        [fixed(arrived.shape)],
        [fixed((rows, width * groups)), fixed((8, 128))],
        [
            jax.ShapeDtypeStruct((rows, width * groups), F32),
            jax.ShapeDtypeStruct((8, 128), F32),
        ],
    )(arrived)
    return shard, square


AXES = ("fsdp", "tp")
PAIR = 2


def swap(value, fsdp_mask, tp_mask, odd_masks=None):
    fsdp_ways, tp_ways = lax.axis_size("fsdp"), lax.axis_size("tp")
    pairs = []
    for row in range(fsdp_ways):
        for col in range(tp_ways):
            masks = (fsdp_mask, tp_mask)
            if odd_masks is not None and col & 1:
                masks = odd_masks
            pairs.append((row * tp_ways + col, (row ^ masks[0]) * tp_ways + (col ^ masks[1])))
    return lax.ppermute(settle(value), AXES, pairs)


def swap_bit(value, axis, bit):
    return swap(value, bit, 0) if axis == "fsdp" else swap(value, 0, bit)


def my_bit(axis, bit):
    return (lax.axis_index(axis) // bit) % 2


def bits_of(ways):
    return [1 << power for power in reversed(range(ways.bit_length() - 1))]


def trade_far(blocks):
    ways = lax.axis_size("fsdp")
    groups = [list(range(side, ways, 2)) for side in range(2)]
    return lax.all_to_all(settle(blocks), "fsdp", 0, 0, axis_index_groups=groups, tiled=True)


def cross(value):
    return swap(value, 1, 0)


def swap_one(value):
    return swap(value, 0, 2, (PAIR, 0))


def swap_two(value):
    return swap(value, PAIR, 0, (0, 2))


def gather_slot(block, other):
    other = settle(other)
    me = lax.axis_index("tp")
    near, far = swap(block, 0, 1), swap(other, 0, 1)
    return arrange([block, other, near, far], [me, me ^ 2, me ^ 1, me ^ 3])


def slot_kernel(x_ref, w_ref, order_ref, *outs):
    rows = outs[0].shape[0]
    place = order_ref[pl.program_id(0)]
    left = x_ref[pl.ds(pl.multiple_of(place * rows, rows), rows), :]
    for number, out_ref in enumerate(outs):

        @pl.when(pl.program_id(0) == number)
        def _(out_ref=out_ref):
            for start in range(0, out_ref.shape[1], TILE):
                here = slice(start, start + TILE)
                out_ref[:, here] = dot_last(left, w_ref[here, :]).astype(BF16)


def slot_product(left, weight):
    me = lax.axis_index("tp")
    rows = left.shape[0] // 4
    cols = weight_shape(weight)[0]
    order = jnp.stack([me ^ 3, me ^ 1, me ^ 2, me]).astype(jnp.int32)
    return run_weights(
        slot_kernel,
        (4,),
        [(fixed(left.shape), left)],
        [weight],
        [(pl.BlockSpec(memory_space=pltpu.SMEM), order)],
        [fixed((rows, cols))] * 4,
        [jax.ShapeDtypeStruct((rows, cols), BF16)] * 4,
    )


def sum_everywhere(value):
    for bit in bits_of(lax.axis_size("tp"))[::-1]:
        value = value + swap(value, 0, bit)
    for bit in bits_of(lax.axis_size("fsdp")):
        value = value + swap(value, bit, 0)
    return value


def on_device(
    tokens,
    out_grad,
    lengths,
    w_query,
    w_key,
    w_value,
    w_out,
    w_gate,
    w_up,
    w_down,
    norm_attn,
    norm_mlp,
    moment_query,
    moment_key,
    moment_value,
    moment_out,
    moment_gate,
    moment_up,
    moment_down,
    moment_norm_attn,
    moment_norm_mlp,
    square_query,
    square_key,
    square_value,
    square_out,
    square_gate,
    square_up,
    square_down,
    square_norm_attn,
    square_norm_mlp,
):
    rows_dev = tokens.shape[0]
    tp_ways = lax.axis_size("tp")
    slot_rows = rows_dev * tp_ways
    heads, heads_kv = w_query.shape[1] // HD, w_key.shape[1] // HD
    shard_rows = w_query.shape[0]
    length = lengths[0]
    row_pos = lax.axis_index("tp") * rows_dev + jnp.arange(rows_dev)
    gain_attn, gain_mlp = norm_attn[None], norm_mlp[None]
    far_rows = shard_rows * (lax.axis_size("fsdp") // 2)

    normed_attn = enter_norm(tokens, gain_attn)
    slot_other = swap(normed_attn, 0, 2)
    qkv_blocks = spread([pin(w_query, normed_attn), w_key, w_value], 1)
    qkv_rows = trade_far(qkv_blocks)
    out_blocks = spread([pin(w_out, qkv_blocks)], 1)
    gate_blocks = spread([pin(w_gate, out_blocks)], 2)
    cosine_table, sine_table = rotary_tables(slot_rows, HD)
    full_qkv = (qkv_rows, cross(qkv_rows))
    cotangent = jnp.where(row_pos[:, None] < length, out_grad, jnp.zeros_like(out_grad))
    grad_pair = swap(cotangent, PAIR, 0)
    attn_input = gather_slot(normed_attn, pin(slot_other, grad_pair))
    out_rows = trade_far(pin(out_blocks, qkv_rows, slot_other))
    full_out = (out_rows, cross(out_rows))
    grad_other, grad_both = swap(cotangent, 0, 2), swap(grad_pair, 0, 2)
    gate_rows = trade_far(pin(gate_blocks, out_rows))

    qkv_rot = project_qkv(pin(attn_input, out_rows), full_qkv, cosine_table, sine_table, heads + heads_kv)
    odd = my_bit("tp", 1)
    grad_mine = arrange(
        [pin(cotangent, qkv_rot), grad_other, grad_pair, grad_both], [0, 1 + odd, 2 - odd, 3]
    )
    grad_near = swap(grad_mine, 0, 1)
    up_blocks = spread([pin(w_up, qkv_rot)], 2)
    attn_bf = attend(pin(qkv_rot, up_blocks), lengths, heads, heads_kv)
    attn_parts = slot_product(pin(attn_bf, grad_mine), full_out)
    attn_got = [swap(part, 0, 1) for part in attn_parts[:2]]
    attn_sent = add_low(rows_dev, (attn_parts[2], 0), (attn_got[0], 0))
    attn_last = swap(attn_sent, 0, 2)
    gate_rows = settle(pin(gate_rows, attn_sent))
    gate_crossed = cross(gate_rows)
    full_gate = (gate_rows, gate_crossed)
    up_rows = trade_far(pin(up_blocks, gate_rows))
    down_blocks = spread([pin(w_down, attn_sent)], 2)
    middle, normed_mlp = middle_norm(
        rows_dev,
        [
            (tokens, 0),
            (attn_parts[3], 0),
            (attn_got[1], 0),
            (pin(attn_last, down_blocks, grad_near), 0),
        ],
        gain_mlp,
    )
    first = swap_one(normed_mlp)
    second = swap_two(normed_mlp)
    up_rows = settle(pin(up_rows, first, gate_crossed))
    up_crossed = cross(up_rows)
    full_up = (up_rows, up_crossed)
    both = swap_two(first)
    mlp_mine = arrange([normed_mlp, first, second, pin(both, up_crossed)], range(4))
    near_blocks = [swap(one, 0, 1) for one in (normed_mlp, first, second)]
    near_blocks.append(swap(pin(both, up_crossed), 0, 1))
    mlp_near = arrange(near_blocks, range(4))
    down_rows = trade_far(pin(down_blocks, up_rows, both, second))
    hid_mine, upp_mine, gatep_mine = mlp_forward(mlp_mine, full_gate, full_up)
    down_rows = settle(pin(down_rows, hid_mine))
    full_down = (down_rows, cross(down_rows))
    hid_near, upp_near, gatep_near = mlp_forward(pin(mlp_near, down_rows), full_gate, full_up)

    down_sent, down_own = weight_grad([grad_mine, grad_near], [hid_mine, hid_near])
    down_got = cross(down_sent)
    dgate_near, dup_near = mlp_backward(pin(grad_near, down_own), full_down, upp_near, gatep_near)
    dgate_mine, dup_mine = mlp_backward(
        pin(grad_mine, dgate_near), full_down, upp_mine, gatep_mine
    )
    gate_sent, gate_own = weight_grad([mlp_mine, mlp_near], [dgate_mine, dgate_near])
    gate_got = cross(gate_sent)
    up_sent, up_own = weight_grad([pin(mlp_mine, gate_own), mlp_near], [dup_mine, dup_near])
    up_got = cross(up_sent)
    down_far = trade_far(add_low(far_rows, (pin(down_got, gate_own), 0), (down_own, 0)))
    back_near = back_product(pin(dgate_near, up_own), dup_near, full_gate, full_up, parts=4)
    back_got = [swap(part, 0, 1) for part in back_near]
    back_mine = back_product(pin(dgate_mine, back_near[0], gate_got), dup_mine, full_gate, full_up, parts=4)
    sent = [add_low(rows_dev, (back_mine[one], 0), (back_got[one], 0)) for one in (2, 3)]
    back_two = [swap_two(one) for one in sent]
    (out_near,) = back_product(pin(hid_near, *sent), full_down)
    (out_mine,) = back_product(pin(hid_mine, out_near), full_down)
    sent = add_low(
        rows_dev, (back_mine[1], 0), (back_got[1], 0), (pin(back_two[1], out_mine, down_far), 0)
    )
    back_one = swap_one(sent)
    out_got = swap(pin(out_near, sent), 0, 1)
    gate_far = trade_far(add_low(far_rows, (pin(gate_got, out_near, down_far), 0), (gate_own, 0)))
    middle_grad, low_grad, gain_mlp_part = leave_norm(
        rows_dev,
        [(back_mine[0], 0), (back_got[0], 0), (back_two[0], 0), (pin(back_one, up_got), 0)],
        middle,
        cotangent,
        gain_mlp,
        [F32, BF16],
    )
    slot_other = swap(low_grad, 0, 2)
    attn_grad_in = gather_slot(low_grad, slot_other)
    proj_sent, proj_own = weight_grad([attn_grad_in], [attn_bf])
    proj_got = cross(proj_sent)
    query_grad, key_grad, value_grad = attend_back(
        pin(attn_grad_in, proj_own, gate_far),
        full_out, qkv_rot, lengths, cosine_table, sine_table, heads, heads_kv,
    )
    up_far = trade_far(add_low(far_rows, (pin(up_got, attn_grad_in, gate_far), 0), (up_own, 0)))
    shard_down, square_down_part = finish_shard(pin(down_far, query_grad), shard_rows, 2)
    sent = add_low(
        2 * rows_dev, (out_mine, 2 * rows_dev), (pin(out_got, query_grad), 2 * rows_dev)
    )
    out_two = swap_two(sent)
    qkv_grad = jnp.concatenate([query_grad, key_grad, value_grad], axis=1)
    qkv_sent, qkv_own = weight_grad([attn_input], [qkv_grad])
    qkv_got = cross(qkv_sent)
    input_parts = slot_product(pin(qkv_grad, qkv_own, proj_got), full_qkv)
    input_got = [swap(part, 0, 1) for part in input_parts[:2]]
    proj_low = add_low(far_rows, (pin(proj_got, up_far, input_parts[3]), 0), (proj_own, 0))
    proj_far = trade_far(proj_low)
    sent = add_low(
        rows_dev, (out_mine, rows_dev), (out_got, rows_dev), (pin(out_two, proj_low), rows_dev)
    )
    out_one = swap_one(sent)
    input_sent = add_low(
        rows_dev, (input_parts[2], 0), (pin(input_got[0], sent, qkv_got), 0)
    )
    input_last = swap(input_sent, 0, 2)
    shard_gate, square_gate_part = finish_shard(pin(gate_far, input_sent), shard_rows, 2)
    shard_up, square_up_part = finish_shard(pin(up_far, input_sent), shard_rows, 2)
    qkv_far = trade_far(add_low(far_rows, (pin(qkv_got, proj_far), 0), (qkv_own, 0)))
    input_grad, gain_attn_part = leave_norm(
        rows_dev,
        [(input_parts[3], 0), (input_got[1], 0), (pin(input_last, shard_gate, shard_up), 0)],
        tokens,
        middle_grad,
        gain_attn,
        [F32],
    )
    block_out = add_low(
        rows_dev,
        (middle, 0),
        (out_mine, 0),
        (out_got, 0),
        (out_two, 0),
        (pin(out_one, input_grad), 0),
    )
    gains = jnp.concatenate([gain_attn_part[0], gain_mlp_part[0]]).reshape(-1, 128)
    shard_out, square_out_part = finish_shard(proj_far, shard_rows, 1)
    shard_qkv, square_qkv_part = finish_shard(pin(qkv_far, block_out), shard_rows, 1)
    width_query, width_key = w_query.shape[1], w_key.shape[1]
    shard_grads = (
        shard_qkv[:, :width_query],
        shard_qkv[:, width_query : width_query + width_key],
        shard_qkv[:, width_query + width_key :],
        shard_out,
        shard_gate,
        shard_up,
        shard_down,
    )
    square_part = (
        square_down_part + square_gate_part + square_up_part + square_qkv_part + square_out_part
    )
    summed = sum_everywhere(jnp.concatenate([gains, square_part]))
    square_total = summed[-1, 0]
    gains = summed[: gains.shape[0]].reshape(-1)
    gain_attn_grad = gains[: norm_attn.shape[0]]
    gain_mlp_grad = gains[norm_attn.shape[0] :]
    clip_norm = jnp.sqrt(
        square_total
        + jnp.sum(gain_attn_grad * gain_attn_grad)
        + jnp.sum(gain_mlp_grad * gain_mlp_grad)
    )
    factor = jnp.minimum(1.0, MAX_NORM / (clip_norm + 1e-06))
    every_grad = tuple(shard_grads) + (gain_attn_grad, gain_mlp_grad)
    params = (w_query, w_key, w_value, w_out, w_gate, w_up, w_down, norm_attn, norm_mlp)
    moments = (
        moment_query,
        moment_key,
        moment_value,
        moment_out,
        moment_gate,
        moment_up,
        moment_down,
        moment_norm_attn,
        moment_norm_mlp,
    )
    squares = (
        square_query,
        square_key,
        square_value,
        square_out,
        square_gate,
        square_up,
        square_down,
        square_norm_attn,
        square_norm_mlp,
    )
    results = [
        adam_step(params[number], every_grad[number], moments[number], squares[number], factor)
        for number in range(9)
    ]
    return (
        block_out,
        input_grad,
        every_grad[0],
        every_grad[1],
        every_grad[2],
        every_grad[3],
        every_grad[4],
        every_grad[5],
        every_grad[6],
        every_grad[7],
        every_grad[8],
        results[0][0],
        results[1][0],
        results[2][0],
        results[3][0],
        results[4][0],
        results[5][0],
        results[6][0],
        results[7][0],
        results[8][0],
        results[0][1],
        results[1][1],
        results[2][1],
        results[3][1],
        results[4][1],
        results[5][1],
        results[6][1],
        results[7][1],
        results[8][1],
        results[0][2],
        results[1][2],
        results[2][2],
        results[3][2],
        results[4][2],
        results[5][2],
        results[6][2],
        results[7][2],
        results[8][2],
        clip_norm,
    )


def solution(mesh):
    return jax.shard_map(
        on_device,
        mesh=mesh,
        in_specs=(
            P(("fsdp", "tp"), None),
            P(("fsdp", "tp"), None),
            P("fsdp"),
            P("fsdp", "tp"),
            P("fsdp", "tp"),
            P("fsdp", "tp"),
            P("fsdp", "tp"),
            P("fsdp", "tp"),
            P("fsdp", "tp"),
            P("fsdp", "tp"),
            P(),
            P(),
            P("fsdp", "tp"),
            P("fsdp", "tp"),
            P("fsdp", "tp"),
            P("fsdp", "tp"),
            P("fsdp", "tp"),
            P("fsdp", "tp"),
            P("fsdp", "tp"),
            P(),
            P(),
            P("fsdp", "tp"),
            P("fsdp", "tp"),
            P("fsdp", "tp"),
            P("fsdp", "tp"),
            P("fsdp", "tp"),
            P("fsdp", "tp"),
            P("fsdp", "tp"),
            P(),
            P(),
        ),
        out_specs=(
            P(("fsdp", "tp"), None),
            P(("fsdp", "tp"), None),
            P("fsdp", "tp"),
            P("fsdp", "tp"),
            P("fsdp", "tp"),
            P("fsdp", "tp"),
            P("fsdp", "tp"),
            P("fsdp", "tp"),
            P("fsdp", "tp"),
            P(),
            P(),
            P("fsdp", "tp"),
            P("fsdp", "tp"),
            P("fsdp", "tp"),
            P("fsdp", "tp"),
            P("fsdp", "tp"),
            P("fsdp", "tp"),
            P("fsdp", "tp"),
            P(),
            P(),
            P("fsdp", "tp"),
            P("fsdp", "tp"),
            P("fsdp", "tp"),
            P("fsdp", "tp"),
            P("fsdp", "tp"),
            P("fsdp", "tp"),
            P("fsdp", "tp"),
            P(),
            P(),
            P("fsdp", "tp"),
            P("fsdp", "tp"),
            P("fsdp", "tp"),
            P("fsdp", "tp"),
            P("fsdp", "tp"),
            P("fsdp", "tp"),
            P("fsdp", "tp"),
            P(),
            P(),
            P(),
        ),
        check_vma=False,
    )
```
